128 devices in a mesh: gx: 4 (over y), gy: 32 (over x, z, core).
Axes of the slice: x: 4, y: 4, z: 4, core: 2. Of those that a mesh axis runs over, the one named last changes fastest.
Arguments:
- blocks: float32 [4, 32, 2, 4, 23, 828], P('gx', 'gy'), may hold values from -1.5 to 1.5, as said below
- halo_members: int32 [4, 32, 28], P('gx', 'gy'), may hold values from -1 to 35, as said below
- chem_potential: float32 [1], replicated, may hold values from -0.8 to 0.8
Outputs:
- density: float32 [4, 32, 4, 23, 828], P('gx', 'gy')
The draws below stay inside these ranges and needn't reach their ends.
Inputs may be any that keep to these rules, and one draw needn't show every extreme that they name: `blocks`: index 0 of the third dimension holds margin rows, index 1 Kohn-Sham rows; every assembled margin submatrix is positive definite. `halo_members`: per device, the used slots come first and hold distinct codes t * 4 + b with t != 4; the rest are -1; at least 14 are used.
All inputs are finite; a program needn't handle non-finite values.
Results may differ from the reference program's by a relative error of at most 0.0003.
Values sent between devices are 32-bit elements; how exact they have to be, the bound alone decides.
No kernel may reach another device: no remote copies, remote signals or barrier semaphores. Data moves between devices by JAX's collectives and lax.ppermute only.
A program may use at most 192 MiB of HBM per device.

```python
import jax
import jax.numpy as jnp
from jax import lax

F = 23
SUBMOL = 32
MT = 4
NS_STEPS = 2
SIGN_STEPS = 3
HALO = 28
NBR = 36
N_GX = 4
N_GY = 32


def draw_blocks(key, part):
    key = jax.random.fold_in(key, 11)
    shape = (N_GX, N_GY, 2, MT, F, NBR * F)
    first_key, second_key = jax.random.split(key, 2)
    kind = lax.broadcasted_iota(jnp.int32, shape, 2)
    molecule = lax.broadcasted_iota(jnp.int32, shape, 3)
    func_row = lax.broadcasted_iota(jnp.int32, shape, 4)
    column = lax.broadcasted_iota(jnp.int32, shape, 5)
    col_code = column // F
    col_func = column % F
    col_tile = col_code // MT
    col_slot = col_code % MT
    same_molecule = col_code == 4 * MT + molecule
    on_diagonal = same_molecule & (col_func == func_row)
    intra = same_molecule & (col_func != func_row)
    partner = (col_tile != 4) & (col_slot == molecule) & (col_func == func_row)
    margin_kind = kind == 0
    intra_limit = jnp.where(margin_kind, 0.4, 3.3) / (F - 1)
    partner_limit = jnp.where(margin_kind, 0.05, 0.6)
    backdrop_limit = jnp.where(margin_kind, 0.12, 0.3) / (NBR * F)
    limit = jnp.where(intra, intra_limit, jnp.where(partner, partner_limit, backdrop_limit))
    off_part = jax.random.uniform(first_key, shape, jnp.float32, -1.0, 1.0) * limit
    level = jax.random.uniform(second_key, shape, jnp.float32, 0.0, 1.0)
    diag_part = jnp.where(margin_kind, 1.0 + 0.5 * level, 3.0 * level - 1.5)
    return jnp.where(on_diagonal, diag_part, off_part).astype(jnp.float32)


def draw_halo_members(key, part):
    key = jax.random.fold_in(key, 23)
    score_key, count_key = jax.random.split(key, 2)
    candidates = 8 * MT
    scores = jax.random.randint(score_key, (N_GX, N_GY, candidates), 0, 1 << 20) * candidates
    scores = scores + jnp.arange(candidates, dtype=jnp.int32)
    ranked = jnp.argsort(scores, axis=-1)[..., :HALO].astype(jnp.int32)
    member_codes = jnp.where(ranked >= 4 * MT, ranked + MT, ranked)
    counts = jax.random.randint(count_key, (N_GX, N_GY, 1), HALO // 2, HALO + 1)
    first_device = (lax.broadcasted_iota(jnp.int32, (N_GX, N_GY, 1), 0) == 0) & (lax.broadcasted_iota(jnp.int32, (N_GX, N_GY, 1), 1) == 0)
    counts = jnp.where(first_device, HALO // 2, counts)
    slots = lax.broadcasted_iota(jnp.int32, (N_GX, N_GY, HALO), 2)
    return jnp.where(slots < counts, member_codes, -1).astype(jnp.int32)


def setup_inputs(seed: int = 0) -> dict:
    streams_of = jax.random.split(jax.random.key(seed), 4)
    return {
        "blocks": draw_blocks(jax.random.fold_in(streams_of[3], 71), 0),
        "halo_members": draw_halo_members(jax.random.fold_in(streams_of[3], 71), 0),
        "chem_potential": jnp.clip(jax.random.uniform(streams_of[2], (1,), jnp.float32, -0.8, 0.8), -0.8, 0.8),
    }


def multiply(former, latter):
    return jnp.dot(former, latter, precision=lax.Precision.HIGHEST, preferred_element_type=jnp.float32)

def row_bound(matrix):
    return jnp.max(lax.optimization_barrier(jnp.sum(jnp.abs(matrix), axis=1)))

def batched_product(former, latter):
    return lax.dot_general(former, latter, (((3,), (2,)), ((0, 1), (0, 1))), precision=lax.Precision.HIGHEST, preferred_element_type=jnp.float32)

def assemble(tile_rows, member_codes):
    in_use = member_codes >= 0
    safe_codes = jnp.where(in_use, member_codes, 0)
    member_tile = safe_codes // MT
    along_x = member_tile // 3 - 1
    along_y = member_tile % 3 - 1
    local_slot = safe_codes % MT
    delta_x = along_x[None, :] - along_x[:, None]
    delta_y = along_y[None, :] - along_y[:, None]
    inside = (jnp.abs(delta_x) <= 1) & (jnp.abs(delta_y) <= 1) & in_use[:, None] & in_use[None, :]
    column_code = (3 * (delta_x + 1) + delta_y + 1) * MT + local_slot[None, :]
    targets = jnp.arange(9 * MT, dtype=jnp.int32)
    selector = ((column_code[:, :, None] == targets[None, None, :]) & inside[:, :, None]).astype(jnp.float32)
    widened = jnp.broadcast_to(selector[:, None], (SUBMOL, F, SUBMOL, 9 * MT))
    joined = []
    for kind in range(2):
        kind_rows = tile_rows[:, kind].reshape(9 * MT, F, 9 * MT, F)
        picked = jnp.take(kind_rows, safe_codes, axis=0)
        joined.append(batched_product(widened, picked).reshape(SUBMOL * F, SUBMOL * F))
    padding = jnp.repeat(1.0 - in_use.astype(jnp.float32), F)
    margin = 0.5 * (joined[0] + joined[0].T) + jnp.diag(padding)
    kohn_sham = 0.5 * (joined[1] + joined[1].T)
    return (margin, kohn_sham)

def density_block(margin, kohn_sham, chem_potential):
    identity = jnp.eye(margin.shape[0], dtype=jnp.float32)
    margin_bound = row_bound(margin)
    scaled = margin / margin_bound
    inverse = identity
    for iteration in range(NS_STEPS):
        factor = 1.5 * identity - 0.5 * multiply(inverse, scaled)
        scaled = multiply(scaled, factor)
        inverse = multiply(factor, inverse)
    inv_root = inverse / jnp.sqrt(margin_bound)
    shifted = kohn_sham - chem_potential[0] * margin
    ortho_ham = multiply(multiply(inv_root, shifted), inv_root)
    sign_iter = ortho_ham / (row_bound(ortho_ham) + 1e-06)
    for iteration in range(SIGN_STEPS):
        sign_iter = multiply(sign_iter, 1.5 * identity - 0.5 * multiply(sign_iter, sign_iter))
    return multiply(multiply(inv_root, identity - sign_iter), inv_root)

def split_density(density, member_codes):
    in_use = member_codes >= 0
    targets = jnp.arange(9 * MT, dtype=jnp.int32)
    placement_map = ((targets[:, None] == member_codes[None, :]) & in_use[None, :]).astype(jnp.float32)
    widened = jnp.broadcast_to(placement_map[None, None], (MT, F, 9 * MT, SUBMOL))
    core_rows = density[:MT * F].reshape(MT, F, SUBMOL, F)
    own_part = batched_product(widened, core_rows).reshape(MT, F, 9 * MT * F)
    core_cols = density[:, :MT * F].reshape(SUBMOL, F * MT * F)
    sent_back = multiply(placement_map, core_cols).reshape(9, MT, F, MT * F)
    return (own_part, sent_back)

def reference(blocks, halo_members, chem_potential):

    def one_device(device):
        row_index = device // N_GY
        col_index = device % N_GY
        pieces = []
        for shift_x in (-1, 0, 1):
            for shift_y in (-1, 0, 1):
                pieces.append(blocks[(row_index + shift_x) % N_GX, (col_index + shift_y) % N_GY])
        tile_rows = jnp.stack(pieces)
        core_codes = 4 * MT + jnp.arange(MT, dtype=jnp.int32)
        member_codes = jnp.concatenate([core_codes, halo_members[row_index, col_index].astype(jnp.int32)])
        margin, kohn_sham = assemble(tile_rows, member_codes)
        density = density_block(margin, kohn_sham, chem_potential)
        return split_density(density, member_codes)
    own_all, back_all = lax.map(one_device, jnp.arange(N_GX * N_GY, dtype=jnp.int32))
    own_all = own_all.reshape(N_GX, N_GY, MT, F, 9 * MT * F)
    back_all = back_all.reshape(N_GX, N_GY, 9, MT, F, MT * F)
    received = []
    for shift_x in (-1, 0, 1):
        for shift_y in (-1, 0, 1):
            source_group = 3 * (1 - shift_x) + (1 - shift_y)
            received.append(jnp.roll(back_all[:, :, source_group], (-shift_x, -shift_y), axis=(0, 1)))
    return 0.5 * (own_all + jnp.concatenate(received, axis=-1))
```

```python
import functools

import jax
import jax.numpy as jnp
from jax import lax
from jax.experimental import pallas as pl
from jax.experimental.pallas import tpu as pltpu
from jax.sharding import PartitionSpec as P

F = 23
G = 24
SUBMOL = 32
MT = 4
TILE = MT * F
DIM = SUBMOL * G
ROWS = MT * G
CODES = 9 * MT
WIDE = 9 * TILE
LANES = 896
EDGE = 640
SHIP = 1408
B = 256
f32 = jnp.float32
bf16 = jnp.bfloat16
VMEM = pl.BlockSpec(memory_space=pltpu.VMEM)
SMEM = pl.BlockSpec(memory_space=pltpu.SMEM)
LIMIT = 48 * 2**20


def params():
    return pltpu.CompilerParams(vmem_limit_bytes=LIMIT)


def dot(a, b):
    return jnp.dot(a, b, preferred_element_type=f32)


def halves(x):
    hi = x.astype(bf16)
    return hi, (x - hi.astype(f32)).astype(bf16)


def pack_kernel(q, blocks_ref, down_ref, up_ref):
    for m in range(MT):
        down_ref[m * G : m * G + F] = blocks_ref[q, m, :, :EDGE]
        down_ref[m * G + F : (m + 1) * G] = jnp.zeros((1, EDGE), f32)
        up_ref[m * G : m * G + F, : WIDE - 256] = blocks_ref[q, m, :, 256:]
        up_ref[m * G : m * G + F, WIDE - 256 :] = jnp.zeros((F, EDGE - WIDE + 256), f32)
        up_ref[m * G + F : (m + 1) * G] = jnp.zeros((1, EDGE), f32)


def rows24(q, blocks_ref, m, width):
    return jnp.concatenate([blocks_ref[q, m, :, :width], jnp.zeros((1, width), f32)], axis=0)


def ship_kernel(q, odd_ref, blocks_ref, plus_ref, minus_ref, cross_ref, inner_ref):
    def packed(up):
        s = TILE * (1 - up)
        o = TILE * up
        own = jnp.concatenate([rows24(q, blocks_ref, m, WIDE) for m in range(MT)], axis=0)
        plus, minus = plus_ref[...], minus_ref[...]
        parts = [own[:, 276 * n + o : 276 * n + o + 184] for n in range(3)]
        parts += [plus[:, 276 * n + o : 276 * n + o + 184] for n in range(2)]
        parts += [minus[:, 276 * n + 20 + o : 276 * n + 20 + o + 184] for n in range(2)]
        tail = SHIP - s - 7 * 184
        if s:
            parts = [jnp.zeros((ROWS, s), f32)] + parts
        return jnp.concatenate(parts + [jnp.zeros((ROWS, tail), f32)], axis=1)

    to_plus, to_minus = packed(1), packed(0)
    odd = odd_ref[0] == 1
    cross_ref[...] = jnp.where(odd, to_plus, to_minus)
    inner_ref[...] = jnp.where(odd, to_minus, to_plus)


def assemble(q, odd_ref, codes_ref, blocks_ref, plus_ref, minus_ref, cross_ref, inner_ref, rows, picked, cols, out, unit):
    for m in range(MT):
        rows[4 * ROWS + m * G : 4 * ROWS + (m + 1) * G, :WIDE] = rows24(q, blocks_ref, m, WIDE)
    plus, minus = plus_ref[...], minus_ref[...]
    zero = lambda w: jnp.zeros((ROWS, w), f32)
    rows[7 * ROWS : 8 * ROWS] = jnp.concatenate([zero(276), plus[:, :552], zero(LANES - 828)], axis=1)
    rows[1 * ROWS : 2 * ROWS] = jnp.concatenate([minus[:, 20:572], zero(LANES - 552)], axis=1)
    odd = odd_ref[0]
    for ref, forward in ((cross_ref, odd), (inner_ref, 1 - odd)):
        v = ref[...]
        lane = lax.broadcasted_iota(jnp.int32, (ROWS, 276), 1) - TILE * forward
        keep = (lane >= 0) & (lane < 184)
        win = lambda a: jnp.where(keep, v[:, a : a + 276], 0.0)
        side = 2 * forward
        own = jnp.concatenate([win(0), win(184), win(368), zero(LANES - 828)], axis=1)
        rows[pl.ds(pl.multiple_of((3 + side) * ROWS, 8), ROWS)] = own
        far = jnp.concatenate([zero(276), win(552), win(736), zero(LANES - 828)], axis=1)
        rows[pl.ds(pl.multiple_of((6 + side) * ROWS, 8), ROWS)] = far
        near = jnp.concatenate([win(920), win(1104), zero(LANES - 552)], axis=1)
        rows[pl.ds(pl.multiple_of(side * ROWS, 8), ROWS)] = near
    for k in range(SUBMOL):
        code = codes_ref[k]
        block = rows[pl.ds(pl.multiple_of(jnp.maximum(code, 0) * G, 8), G)]
        picked[k * G : (k + 1) * G] = jnp.where(code >= 0, block, 0.0)
    for c in range(LANES // 128):
        for j in range(DIM // 128):
            cols[j, 128 * c : 128 * (c + 1)] = picked[128 * j : 128 * (j + 1), 128 * c : 128 * (c + 1)].T
    row = lax.broadcasted_iota(jnp.int32, (G, 128), 0)
    lane = lax.broadcasted_iota(jnp.int32, (G, 128), 1)
    for k in range(SUBMOL):
        code = codes_ref[k]
        start = jnp.maximum(code, 0) * F
        for j in range(DIM // 128):
            block = cols[j, pl.ds(start, G)]
            if unit:
                other = jnp.where(lane + 128 * j == row + G * k, 1.0, 0.0)
            else:
                other = jnp.zeros((G, 128), f32)
            picked[k * G : (k + 1) * G, 128 * j : 128 * (j + 1)] = jnp.where(
                code >= 0, jnp.where(row < F, block, 0.0), other
            )
    for i in range(3):
        for j in range(i, 3):
            a, b = slice(B * i, B * i + B), slice(B * j, B * j + B)
            mean = 0.5 * (picked[a, b] + picked[b, a].T)
            out[a, b] = mean
            if j > i:
                out[b, a] = mean.T


def put_halves(x, hi_ref, lo_ref):
    hi_ref[...], lo_ref[...] = halves(x)


def product(ah, al, bh, bl, out):
    for j in range(3):
        c = slice(B * j, B * j + B)
        out[:, c] = dot(ah[...], bh[:, c]) + dot(ah[...], bl[:, c]) + dot(al[...], bh[:, c])


def symmetric_product(ah, al, bh, bl, out):
    for j in range(3):
        c = slice(B * j, B * j + B)
        r = B * (j + 1)
        block = dot(ah[:r], bh[:, c]) + dot(ah[:r], bl[:, c]) + dot(al[:r], bh[:, c])
        out[:r, c] = block
        for i in range(j):
            out[c, B * i : B * i + B] = block[B * i : B * i + B].T


def bound_of(matrix):
    return jnp.max(jnp.sum(jnp.abs(matrix), axis=0, keepdims=True))


def eye():
    return (
        lax.broadcasted_iota(jnp.int32, (DIM, DIM), 0) == lax.broadcasted_iota(jnp.int32, (DIM, DIM), 1)
    ).astype(f32)


def margin_kernel(
    odd_ref, codes_ref, blocks_ref, plus_ref, minus_ref, cross_ref, inner_ref,
    margin_ref, root_hi, root_lo, rows, picked, cols, hi, lo, y,
):
    assemble(0, odd_ref, codes_ref, blocks_ref, plus_ref, minus_ref, cross_ref, inner_ref, rows, picked, cols, margin_ref, True)
    margin = margin_ref[...]
    bound = bound_of(margin)
    scaled = margin / bound
    y[...] = scaled
    put_halves(scaled, hi, lo)
    work = picked.at[:, :DIM]
    symmetric_product(hi, lo, hi, lo, work)
    put_halves(work[...] - 4.5 * y[...] + 3.375 * eye(), hi, lo)
    symmetric_product(hi, lo, hi, lo, work)
    factor = lax.rsqrt(jnp.full((1, DIM), bound, f32)) * 0.0625
    put_halves((work[...] - 8.625 * y[...] + 24.609375 * eye()) * factor, root_hi, root_lo)


def density_kernel(
    odd_ref, codes_ref, chem_ref, blocks_ref, plus_ref, minus_ref, cross_ref, inner_ref,
    margin_ref, root_hi, root_lo, w_ref, wt_ref, rows, picked, cols, hi, lo, hi2, lo2, ham, narrow, tall,
):
    assemble(1, odd_ref, codes_ref, blocks_ref, plus_ref, minus_ref, cross_ref, inner_ref, rows, picked, cols, ham, False)
    put_halves(ham[...] - chem_ref[0] * margin_ref[...], hi, lo)
    work = picked.at[:, :DIM]
    product(root_hi, root_lo, hi, lo, work)
    put_halves(work[...], hi, lo)
    symmetric_product(hi, lo, root_hi, root_lo, ham)
    bound = bound_of(ham[...]) + 1e-06
    put_halves(ham[...] / bound, hi, lo)
    symmetric_product(hi, lo, hi, lo, work)
    put_halves(1.5 * eye() - 0.5 * work[...], hi2, lo2)
    symmetric_product(hi, lo, hi2, lo2, work)
    put_halves(work[...], hi, lo)

    def thin(v, bh, bl):
        vh, vl = halves(v)
        both = jnp.concatenate([vh, vl], axis=0)
        whole = dot(both, bh[...])
        return whole[:ROWS] + whole[ROWS:] + dot(vh, bl[...])

    def once(v):
        return thin(v, hi, lo)

    def second(v):
        return once(1.5 * v - 0.5 * once(once(v)))

    core = root_hi[:ROWS].astype(f32) + root_lo[:ROWS].astype(f32)
    inner = 1.5 * core - 0.5 * second(second(core))
    density = thin(core - second(inner), root_hi, root_lo)

    narrow[...] = jnp.zeros((128, DIM), f32)
    for m in range(MT):
        narrow[m * F : (m + 1) * F] = density[m * G : m * G + F]
    for j in range(DIM // 128):
        tall[128 * j : 128 * (j + 1)] = narrow[:, 128 * j : 128 * (j + 1)].T
    wt_ref[...] = jnp.zeros((CODES * G, 128), f32)
    for k in range(SUBMOL):
        code = codes_ref[k]

        @pl.when(code >= 0)
        def _():
            wt_ref[pl.ds(pl.multiple_of(code * G, 8), G)] = tall[k * G : (k + 1) * G]

    for c in range(CODES):
        cols[0, c * F : c * F + G] = wt_ref[c * G : (c + 1) * G]
    cols[0, WIDE:LANES] = jnp.zeros((LANES - WIDE, 128), f32)
    for c in range(LANES // 128):
        w_ref[:, 128 * c : 128 * (c + 1)] = cols[0, 128 * c : 128 * (c + 1)].T


def final_kernel(odd_ref, w_ref, tile_ref, up_ref, down_ref, cross_ref, inner_ref, out_ref):
    odd = odd_ref[0] == 1
    plus = [jnp.where(odd, cross_ref[n], inner_ref[n])[:, :TILE] for n in range(3)]
    minus = [jnp.where(odd, inner_ref[n], cross_ref[n])[:, :TILE] for n in range(3)]
    received = jnp.concatenate(
        [
            minus[1], up_ref[:, :TILE], plus[1],
            minus[0], tile_ref[:, :TILE], plus[0],
            minus[2], down_ref[:, :TILE], plus[2],
        ],
        axis=1,
    )
    for m in range(MT):
        out_ref[m] = 0.5 * (w_ref[m * F : (m + 1) * F, :WIDE] + received[m * G : m * G + F])


def struct(shape, dtype=f32):
    return jax.ShapeDtypeStruct(shape, dtype)


def shards(blocks, halo_members, chem_potential):
    n_x, n_y = lax.axis_size("gx"), lax.axis_size("gy")
    ahead = [(i, (i + 1) % n_x) for i in range(n_x)]
    back = [((i + 1) % n_x, i) for i in range(n_x)]
    crossing = [(j, (j + 1) % n_y if j % 2 else (j - 1) % n_y) for j in range(n_y)]
    inside = [(j, j ^ 1) for j in range(n_y)]
    odd = (lax.axis_index("gy") % 2).astype(jnp.int32).reshape(1)
    codes = jnp.concatenate([4 * MT + jnp.arange(MT, dtype=jnp.int32), halo_members[0, 0]])
    blocks = blocks[0, 0]

    plus, minus, cross, inner = [], [], [], []
    for q in range(2):
        down, up = pl.pallas_call(
            functools.partial(pack_kernel, q),
            out_shape=[struct((ROWS, EDGE))] * 2,
            in_specs=[VMEM],
            out_specs=[VMEM] * 2,
            name=f"pack{q}",
            compiler_params=params(),
        )(blocks)
        plus.append(lax.ppermute(down, "gx", back))
        minus.append(lax.ppermute(up, "gx", ahead))
    for q in range(2):
        x, i = pl.pallas_call(
            functools.partial(ship_kernel, q),
            out_shape=[struct((ROWS, SHIP))] * 2,
            in_specs=[SMEM, VMEM, VMEM, VMEM],
            out_specs=[VMEM] * 2,
            name=f"ship{q}",
            compiler_params=params(),
        )(odd, blocks, plus[q], minus[q])
        cross.append(lax.ppermute(x, "gy", crossing))
        inner.append(lax.ppermute(i, "gy", inside))
    work = [
        pltpu.VMEM((CODES * G, LANES), f32),
        pltpu.VMEM((DIM, LANES), f32),
        pltpu.VMEM((DIM // 128, LANES, 128), f32),
        pltpu.VMEM((DIM, DIM), bf16),
        pltpu.VMEM((DIM, DIM), bf16),
    ]
    margin, root_hi, root_lo = pl.pallas_call(
        margin_kernel,
        out_shape=[struct((DIM, DIM)), struct((DIM, DIM), bf16), struct((DIM, DIM), bf16)],
        in_specs=[SMEM, SMEM, VMEM] + [VMEM] * 4,
        out_specs=[VMEM] * 3,
        scratch_shapes=work + [pltpu.VMEM((DIM, DIM), f32)],
        name="inverse_root",
        compiler_params=params(),
        cost_estimate=pl.CostEstimate(flops=4 * 2 * DIM**3, bytes_accessed=2**23, transcendentals=0),
    )(odd, codes, blocks, plus[0], minus[0], cross[0], inner[0])
    w, tiles = pl.pallas_call(
        density_kernel,
        out_shape=[struct((128, LANES)), struct((CODES * G, 128))],
        in_specs=[SMEM, SMEM, SMEM, VMEM] + [VMEM] * 7,
        out_specs=[VMEM] * 2,
        scratch_shapes=work
        + [
            pltpu.VMEM((DIM, DIM), bf16),
            pltpu.VMEM((DIM, DIM), bf16),
            pltpu.VMEM((DIM, DIM), f32),
            pltpu.VMEM((128, DIM), f32),
            pltpu.VMEM((DIM, 128), f32),
        ],
        name="density",
        compiler_params=params(),
        cost_estimate=pl.CostEstimate(flops=12 * 2 * DIM**3, bytes_accessed=2**23, transcendentals=0),
    )(odd, codes, chem_potential, blocks, plus[1], minus[1], cross[1], inner[1], margin, root_hi, root_lo)
    tiles = tiles.reshape(9, ROWS, 128)
    from_minus = lax.ppermute(tiles[6:9], "gx", ahead)
    from_plus = lax.ppermute(tiles[0:3], "gx", back)
    to_plus = jnp.stack([tiles[5], from_minus[2], from_plus[2]])
    to_minus = jnp.stack([tiles[3], from_minus[0], from_plus[0]])
    is_odd = odd[0] == 1
    x = lax.ppermute(jnp.where(is_odd, to_plus, to_minus), "gy", crossing)
    i = lax.ppermute(jnp.where(is_odd, to_minus, to_plus), "gy", inside)
    out = pl.pallas_call(
        final_kernel,
        out_shape=struct((MT, F, WIDE)),
        in_specs=[SMEM] + [VMEM] * 6,
        out_specs=VMEM,
        name="symmetrize",
        compiler_params=params(),
    )(odd, w, tiles[4], from_minus[1], from_plus[1], x, i)
    return out[None, None]


def solution(mesh):
    return jax.shard_map(
        shards,
        mesh=mesh,
        in_specs=(P("gx", "gy", None, None, None, None), P("gx", "gy", None), P()),
        out_specs=P("gx", "gy", None, None, None),
        check_vma=False,
    )
```

```python
import functools

import jax
import jax.numpy as jnp
from jax import lax
from jax.experimental import pallas as pl
from jax.experimental.pallas import tpu as pltpu
from jax.sharding import PartitionSpec as P

F = 23
G = 24
SUBMOL = 32
MT = 4
TILE = MT * F
DIM = SUBMOL * G
ROWS = MT * G
CODES = 9 * MT
WIDE = 9 * TILE
LANES = 896
EDGE = 640
SIDE = 1152
CORNER = 768
NEAR = 640
ZERO = 840
B = 256
f32 = jnp.float32
bf16 = jnp.bfloat16
VMEM = pl.BlockSpec(memory_space=pltpu.VMEM)
SMEM = pl.BlockSpec(memory_space=pltpu.SMEM)
LIMIT = 32 * 2**20


def params():
    return pltpu.CompilerParams(vmem_limit_bytes=LIMIT)


def dot(a, b):
    return jnp.dot(a, b, preferred_element_type=f32)


def halves(x):
    hi = x.astype(bf16)
    return hi, (x - hi.astype(f32)).astype(bf16)


def fold(v, ref):
    whole = ref.shape[1]
    rest = v.shape[1] - whole
    each = 12 * 128 // whole
    parts = []
    for g in range(12):
        parts.append(v[8 * g : 8 * (g + 1), whole:])
        if (g + 1) % each == 0:
            parts.append(jnp.zeros((8, 128 - each * rest), f32))
    ref[:ROWS] = v[:, :whole]
    ref[ROWS:] = jnp.concatenate(parts, axis=1)


def unfold(ref, rest):
    each = 12 * 128 // ref.shape[1]
    starts = [128 * (g // each) + rest * (g % each) for g in range(12)]
    last = jnp.concatenate([ref[ROWS : ROWS + 8, a : a + rest] for a in starts], axis=0)
    return jnp.concatenate([ref[:ROWS], last], axis=1)


def pack_kernel(q, blocks_ref, down_ref, up_ref, own_ref, held, sems):
    cuts = (0, 6, 12, 18, F)
    copies = []
    for n in range(4):
        f = pl.ds(cuts[n], cuts[n + 1] - cuts[n])
        copies.append(pltpu.make_async_copy(blocks_ref.at[q, f], held.at[f], sems.at[n]))
    for copy in copies:
        copy.start()
    for copy in copies:
        copy.wait()
    parts = [held[f] for f in range(F)] + [jnp.zeros((MT, WIDE), f32)]
    own = jnp.concatenate(parts, axis=0)
    own_ref[:, :WIDE] = own
    own_ref[:, WIDE:] = jnp.zeros((ROWS, LANES - WIDE), f32)
    down_ref[...] = own[:, :EDGE]
    up_ref[...] = jnp.concatenate([own[:, 276:], blank(EDGE - 552)], axis=1)


def blank(width):
    return jnp.zeros((ROWS, width), f32)


def side_kernel(odd_ref, margin_ref, ham_ref, cross_ref):
    def packed(o):
        parts = [ref[:, 276 * n + o : 276 * n + o + 184] for ref in (margin_ref, ham_ref) for n in range(3)]
        return jnp.concatenate(parts + [blank(SIDE - 6 * 184)], axis=1)

    cross_ref[...] = jnp.where(odd_ref[0] == 1, packed(TILE), packed(0))


def corner_kernel(odd_ref, own_ref, plus_ref, minus_ref, cross_ref, inner_ref, near_ref):
    rows = (plus_ref[:, :552], minus_ref[:, :552])
    own = own_ref[...]

    def packed(o):
        parts = [v[:, 276 * n + o : 276 * n + o + 184] for v in rows for n in range(2)]
        return jnp.concatenate(parts + [blank(CORNER - 184 * 4)], axis=1)

    def near(o):
        parts = [own[:, 276 * n + o : 276 * n + o + 184] for n in range(3)]
        return jnp.concatenate(parts + [blank(NEAR - 184 * 3)], axis=1)

    odd = odd_ref[0] == 1
    to_plus, to_minus = packed(TILE), packed(0)
    cross_ref[...] = jnp.where(odd, to_plus, to_minus)
    inner_ref[...] = jnp.where(odd, to_minus, to_plus)
    near_ref[...] = jnp.where(odd, near(0), near(TILE))


def put(block, at, hi_ref, lo_ref):
    hi = block.astype(bf16)
    hi_ref[at] = hi
    lo_ref[at] = (block - hi.astype(f32)).astype(bf16)


def diagonal(rows, shift):
    row = lax.broadcasted_iota(jnp.int32, (rows, B), 0)
    return row == lax.broadcasted_iota(jnp.int32, (rows, B), 1) + shift


def part(i):
    return slice(B * i, B * (i + 1))


def column_sums(matrix):
    return jnp.sum(jnp.abs(matrix), axis=0, keepdims=True)


def largest(sums):
    return jnp.max(jnp.maximum(jnp.maximum(sums[0], sums[1]), sums[2]))


def assemble(q, odd_ref, codes_ref, own_ref, plus_ref, minus_ref, side_ref, cross_ref, inner_ref, near_ref, work, unit, sink):
    rows, picked, cols = work

    def set_rows(t, v):
        for c in range(LANES // 128):
            rows[c, t * ROWS : (t + 1) * ROWS] = v[:, 128 * c : 128 * (c + 1)]

    set_rows(4, own_ref[...])
    set_rows(7, jnp.concatenate([blank(276), plus_ref[:, :552], blank(LANES - 828)], axis=1))
    set_rows(1, jnp.concatenate([minus_ref[:, :552], blank(LANES - 552)], axis=1))
    set_rows(9, blank(LANES))

    def place(side_ref, begin, corner_ref, ahead):
        gap = TILE * ahead
        for base, ref, first, count, left in (
            (3, side_ref, begin, 3, 0), (6, corner_ref, 0, 2, 276), (0, corner_ref, 368, 2, 0),
        ):
            parts = [blank(left + gap)] if left + gap else []
            for n in range(count):
                parts += [ref[:, first + 184 * n : first + 184 * (n + 1)], blank(TILE)]
            parts[-1] = blank(LANES - left - gap - 276 * count + TILE)
            set_rows(base + 2 * ahead, jnp.concatenate(parts, axis=1))

    @pl.when(odd_ref[0] == 1)
    def _():
        place(side_ref, 552 * q, cross_ref, 1)
        place(near_ref, 0, inner_ref, 0)

    @pl.when(odd_ref[0] != 1)
    def _():
        place(side_ref, 552 * q, cross_ref, 0)
        place(near_ref, 0, inner_ref, 1)

    codes = [codes_ref[k] for k in range(SUBMOL)]
    begin = [jnp.where(c >= 0, (c >> 2) * ROWS + (c & 3), 9 * ROWS) for c in codes]
    for c in range(LANES // 128):
        for h in range(2):
            slots = range(16 * h, 16 * (h + 1))
            turned = jnp.concatenate([rows[c, pl.ds(begin[k], G, stride=MT)] for k in slots], axis=0).T
            for j in range(3):
                cols[3 * h + j, 128 * c : 128 * (c + 1)] = turned[:, 128 * j : 128 * (j + 1)]
    begin = [jnp.where(c >= 0, c * F, ZERO) for c in codes]
    row = lax.broadcasted_iota(jnp.int32, (8, 128), 0)
    lane = lax.broadcasted_iota(jnp.int32, (G, 128), 1)
    line = lax.broadcasted_iota(jnp.int32, (G, 128), 0)
    for k in range(SUBMOL):
        for j in range(DIM // 128):
            block = cols[j, pl.ds(begin[k], G)]
            block = jnp.concatenate([block[:16], jnp.where(row < 7, block[16:], 0.0)], axis=0)
            if unit and G * k < 128 * (j + 1) and G * (k + 1) > 128 * j:
                ones = jnp.where(lane + 128 * j == line + G * k, 1.0, 0.0)
                block = jnp.where(codes[k] >= 0, block, ones)
            picked[k * G : (k + 1) * G, 128 * j : 128 * (j + 1)] = block
    for i in range(3):
        for j in range(i, 3):
            sink(i, j, 0.5 * (picked[part(i), part(j)] + picked[part(j), part(i)].T))


def symmetric_product(ah, al, bh, bl, sink):
    for j in range(3):
        c = part(j)
        r = B * (j + 1)
        block = dot(ah[:r], bh[:, c]) + dot(ah[:r], bl[:, c]) + dot(al[:r], bh[:, c])
        for i in range(j + 1):
            sink(i, j, block[part(i)])


def put_both(i, j, block, hi_ref, lo_ref):
    put(block, (part(i), part(j)), hi_ref, lo_ref)
    if i < j:
        put(block.T, (part(j), part(i)), hi_ref, lo_ref)


def root_kernel(
    odd_ref, codes_ref, own_ref, plus_ref, minus_ref, side_ref, cross_ref, inner_ref, near_ref,
    margin_ref, root_hi, root_lo, rows, picked, cols, hi, lo, hi2, lo2,
):
    sums = [jnp.zeros((1, B), f32)] * 3

    def first(i, j, block):
        margin_ref[part(i), part(j)] = block
        put_both(i, j, block, hi, lo)
        sums[j] += column_sums(block)
        if i < j:
            other = block.T
            margin_ref[part(j), part(i)] = other
            sums[i] += column_sums(other)

    assemble(
        0, odd_ref, codes_ref, own_ref, plus_ref, minus_ref, side_ref, cross_ref, inner_ref, near_ref,
        (rows, picked, cols), True, first,
    )
    bound = largest(sums)
    one = 1.0 / jnp.full((1, B), bound, f32)
    two = one * one
    root = lax.rsqrt(jnp.full((1, B), bound, f32)) * 0.0625

    def second(i, j, block):
        value = block * two - (4.5 * one) * margin_ref[part(i), part(j)]
        if i == j:
            value = value + jnp.where(diagonal(B, 0), 3.375, 0.0)
        put_both(i, j, value, hi2, lo2)

    symmetric_product(hi, lo, hi, lo, second)

    def third(i, j, block):
        value = block - (8.625 * one) * margin_ref[part(i), part(j)]
        if i == j:
            value = value + jnp.where(diagonal(B, 0), 24.609375, 0.0)
        put_both(i, j, value * root, root_hi, root_lo)

    symmetric_product(hi2, lo2, hi2, lo2, third)


def density_kernel(
    odd_ref, codes_ref, chem_ref, own_ref, plus_ref, minus_ref, side_ref, cross_ref, inner_ref, near_ref,
    margin_ref, root_hi, root_lo, spread, up_ref, mid_ref, down_ref,
    rows, picked, cols, hi, lo, hi2, lo2, hi3, lo3, narrow, tall, pieces,
):
    chem = chem_ref[0]

    def first(i, j, block):
        put_both(i, j, block - chem * margin_ref[part(i), part(j)], hi, lo)

    assemble(
        1, odd_ref, codes_ref, own_ref, plus_ref, minus_ref, side_ref, cross_ref, inner_ref, near_ref,
        (rows, picked, cols), False, first,
    )
    for j in range(3):
        c = part(j)
        half = dot(root_hi[...], hi[:, c]) + dot(root_hi[...], lo[:, c]) + dot(root_lo[...], hi[:, c])
        put(half, (slice(None), c), hi2, lo2)
    sums = [jnp.zeros((1, B), f32)] * 3

    def second(i, j, block):
        put(block, (part(i), part(j)), hi, lo)
        sums[j] += column_sums(block)
        if i < j:
            other = block.T
            put(other, (part(j), part(i)), hi, lo)
            sums[i] += column_sums(other)

    symmetric_product(hi2, lo2, root_hi, root_lo, second)
    scale = 1.0 / jnp.full((1, B), largest(sums) + 1e-06, f32)
    half_two = 0.5 * (scale * scale)

    def third(i, j, block):
        value = -half_two * block
        if i == j:
            value = value + jnp.where(diagonal(B, 0), 1.5, 0.0)
        put_both(i, j, value, hi2, lo2)

    symmetric_product(hi, lo, hi, lo, third)

    def fourth(i, j, block):
        put_both(i, j, block * scale, hi3, lo3)

    symmetric_product(hi, lo, hi2, lo2, fourth)

    def thin(v, bh, bl):
        vh, vl = halves(v)
        both = jnp.concatenate([vh, vl], axis=0)
        whole = dot(both, bh[...])
        return whole[:ROWS] + whole[ROWS:] + dot(vh, bl[...])

    def once(v):
        return thin(v, hi3, lo3)

    def next_sign(v):
        return once(1.5 * v - 0.5 * once(once(v)))

    core = root_hi[:ROWS].astype(f32) + root_lo[:ROWS].astype(f32)
    inside = 1.5 * core - 0.5 * next_sign(next_sign(core))
    density = thin(core - next_sign(inside), root_hi, root_lo)

    narrow[...] = jnp.zeros((128, DIM), f32)
    for m in range(MT):
        narrow[m * F : (m + 1) * F] = density[m * G : m * G + F]
    for j in range(DIM // 128):
        tall[128 * j : 128 * (j + 1)] = narrow[:, 128 * j : 128 * (j + 1)].T
    spread[...] = jnp.zeros((CODES * G, 128), f32)
    for k in range(SUBMOL):
        code = codes_ref[k]

        @pl.when(code >= 0)
        def _():
            spread[pl.ds(pl.multiple_of(code * G, 8), G)] = tall[k * G : (k + 1) * G]

    odd = odd_ref[0]
    for dx, ref in ((-1, down_ref), (0, mid_ref), (1, up_ref)):
        for dy in (-1, 0, 1):
            place = 1 + dy - 2 * dy * odd
            t = 3 * (dx + 1) + dy + 1
            for m in range(MT):
                block = spread[t * ROWS + m * G : t * ROWS + m * G + F]
                pieces[place, pl.ds(m, F, stride=MT)] = block
            pieces[place, MT * F :] = jnp.zeros((ROWS - MT * F, 128), f32)
        v = jnp.concatenate([pieces[n][:, :TILE] for n in range(3)], axis=1)
        if dx:
            fold(v, ref)
        else:
            ref[...] = v


def own_kernel(spread, w_ref, flat):
    for c in range(CODES):
        flat[c * F : c * F + G] = spread[c * G : (c + 1) * G]
    flat[WIDE:LANES] = jnp.zeros((LANES - WIDE, 128), f32)
    for c in range(LANES // 128):
        own = flat[128 * c : 128 * (c + 1)].T
        for m in range(MT):
            w_ref[c, pl.ds(m, F, stride=MT)] = own[m * F : (m + 1) * F]
        w_ref[c, MT * F :] = jnp.zeros((ROWS - MT * F, 128), f32)


def turn_kernel(mid_ref, up_ref, down_ref, cross_ref, inner_ref):
    rows = (mid_ref[...], unfold(up_ref, 20), unfold(down_ref, 20))
    fold(jnp.concatenate([v[:, :TILE] for v in rows], axis=1), cross_ref)
    fold(jnp.concatenate([v[:, 2 * TILE :] for v in rows], axis=1), inner_ref)


def final_kernel(odd_ref, w_ref, mid_ref, up_ref, down_ref, cross_ref, inner_ref, out_ref):
    odd = odd_ref[0] == 1
    cross, inner = unfold(cross_ref, 20), unfold(inner_ref, 20)
    plus = jnp.where(odd, cross, inner)
    minus = jnp.where(odd, inner, cross)
    middle = (mid_ref[...], unfold(up_ref, 20), unfold(down_ref, 20))
    parts = []
    for n in (1, 0, 2):
        parts += [v[:, TILE * k : TILE * (k + 1)] for v, k in ((minus, n), (middle[n], 1), (plus, n))]
    received = jnp.concatenate(parts, axis=1)
    own = jnp.concatenate([w_ref[c] for c in range(LANES // 128)], axis=1)
    whole = 0.5 * (own[: MT * F, :WIDE] + received[: MT * F])
    for g in range(F):
        out_ref[g] = whole[MT * g : MT * (g + 1)]


def struct(shape, dtype=f32):
    return jax.ShapeDtypeStruct(shape, dtype)


def shards(blocks, halo_members, chem_potential):
    n_x, n_y = lax.axis_size("gx"), lax.axis_size("gy")
    ahead = [(i, (i + 1) % n_x) for i in range(n_x)]
    back = [((i + 1) % n_x, i) for i in range(n_x)]
    crossing = [(j, (j + 1) % n_y if j % 2 else (j - 1) % n_y) for j in range(n_y)]
    inside = [(j, j ^ 1) for j in range(n_y)]
    odd = (lax.axis_index("gy") % 2).astype(jnp.int32).reshape(1)
    codes = jnp.concatenate([4 * MT + jnp.arange(MT, dtype=jnp.int32), halo_members[0, 0]])
    ANY = pl.BlockSpec(memory_space=pltpu.HBM)
    native = pltpu.with_memory_space_constraint(jnp.transpose(blocks[0, 0], (0, 2, 1, 3)), pltpu.HBM)

    plus, minus, own = [], [], []
    for q in range(2):
        down, up, mine = pl.pallas_call(
            functools.partial(pack_kernel, q),
            out_shape=[struct((ROWS, EDGE)), struct((ROWS, EDGE)), struct((ROWS, LANES))],
            in_specs=[ANY],
            out_specs=[VMEM] * 3,
            scratch_shapes=[pltpu.VMEM((F, MT, WIDE), f32), pltpu.SemaphoreType.DMA((4,))],
            name=f"pack{q}",
            compiler_params=params(),
        )(native)
        plus.append(lax.ppermute(down, "gx", back))
        minus.append(lax.ppermute(up, "gx", ahead))
        own.append(mine)
    side = pl.pallas_call(
        side_kernel,
        out_shape=struct((ROWS, SIDE)),
        in_specs=[SMEM, VMEM, VMEM],
        out_specs=VMEM,
        name="side",
        compiler_params=params(),
    )(odd, *own)
    side = lax.ppermute(side, "gy", crossing)
    corners = []
    for q in range(2):
        x, i, near = pl.pallas_call(
            corner_kernel,
            out_shape=[struct((ROWS, CORNER)), struct((ROWS, CORNER)), struct((ROWS, NEAR))],
            in_specs=[SMEM, VMEM, VMEM, VMEM],
            out_specs=[VMEM] * 3,
            name=f"corner{q}",
            compiler_params=params(),
            cost_estimate=pl.CostEstimate(flops=(0, 40000000000)[q], bytes_accessed=(1, 10**8)[q], transcendentals=0),
        )(odd, own[q], plus[q], minus[q])
        corners.append(
            (lax.ppermute(x, "gy", crossing), lax.ppermute(i, "gy", inside), lax.ppermute(near, "gy", inside))
        )
    square = pltpu.VMEM((DIM, DIM), bf16)
    work = [
        pltpu.VMEM((LANES // 128, 10 * ROWS, 128), f32),
        pltpu.VMEM((DIM, DIM), f32),
        pltpu.VMEM((DIM // 128, LANES, 128), f32),
    ]
    margin, root_hi, root_lo = pl.pallas_call(
        root_kernel,
        out_shape=[struct((DIM, DIM)), struct((DIM, DIM), bf16), struct((DIM, DIM), bf16)],
        in_specs=[SMEM, SMEM] + [VMEM] * 7,
        out_specs=[VMEM] * 3,
        scratch_shapes=work + [square] * 4,
        name="inverse_root",
        compiler_params=params(),
        cost_estimate=pl.CostEstimate(flops=4 * 2 * DIM**3, bytes_accessed=2**23, transcendentals=0),
    )(odd, codes, own[0], plus[0], minus[0], side, *corners[0])
    folded = struct((ROWS + 8, 256))
    spread, up, mid, down = pl.pallas_call(
        density_kernel,
        out_shape=[struct((CODES * G, 128)), folded, struct((ROWS, 3 * TILE)), folded],
        in_specs=[SMEM, SMEM, SMEM] + [VMEM] * 10,
        out_specs=[VMEM] * 4,
        scratch_shapes=work
        + [square] * 6
        + [pltpu.VMEM((128, DIM), f32), pltpu.VMEM((DIM, 128), f32), pltpu.VMEM((3, ROWS, 128), f32)],
        name="density",
        compiler_params=params(),
        cost_estimate=pl.CostEstimate(flops=12 * 2 * DIM**3, bytes_accessed=2**23, transcendentals=0),
    )(odd, codes, chem_potential, own[1], plus[1], minus[1], side, *corners[1], margin, root_hi, root_lo)
    from_minus = lax.ppermute(up, "gx", ahead)
    from_plus = lax.ppermute(down, "gx", back)
    w = pl.pallas_call(
        own_kernel,
        out_shape=struct((LANES // 128, ROWS, 128)),
        in_specs=[VMEM],
        out_specs=VMEM,
        scratch_shapes=[pltpu.VMEM((LANES, 128), f32)],
        name="own",
        compiler_params=params(),
    )(spread)
    x, i = pl.pallas_call(
        turn_kernel,
        out_shape=[folded] * 2,
        in_specs=[VMEM] * 3,
        out_specs=[VMEM] * 2,
        name="turn",
        compiler_params=params(),
    )(mid, from_minus, from_plus)
    x = lax.ppermute(x, "gy", crossing)
    i = lax.ppermute(i, "gy", inside)
    out = pl.pallas_call(
        final_kernel,
        out_shape=struct((F, MT, WIDE)),
        in_specs=[SMEM] + [VMEM] * 6,
        out_specs=VMEM,
        name="symmetrize",
        compiler_params=params(),
    )(odd, w, mid, from_minus, from_plus, x, i)
    return jnp.transpose(out, (1, 0, 2))[None, None]


def solution(mesh):
    return jax.shard_map(
        shards,
        mesh=mesh,
        in_specs=(P("gx", "gy", None, None, None, None), P("gx", "gy", None), P()),
        out_specs=P("gx", "gy", None, None, None),
        check_vma=False,
    )
```

```python
import functools

import jax
import jax.numpy as jnp
from jax import lax
from jax.experimental import pallas as pl
from jax.experimental.pallas import tpu as pltpu
from jax.sharding import PartitionSpec as P

F = 23
G = 24
SUBMOL = 32
MT = 4
TILE = MT * F
DIM = SUBMOL * G
ROWS = MT * G
CODES = 9 * MT
WIDE = 9 * TILE
LANES = 896
EDGE = 640
SIDE = 1152
CORNER = 768
NEAR = 640
ZERO = 840
B = 256
f32 = jnp.float32
bf16 = jnp.bfloat16
VMEM = pl.BlockSpec(memory_space=pltpu.VMEM)
SMEM = pl.BlockSpec(memory_space=pltpu.SMEM)
LIMIT = 32 * 2**20


def params():
    return pltpu.CompilerParams(vmem_limit_bytes=LIMIT)


def dot(a, b):
    return jnp.dot(a, b, preferred_element_type=f32)


def halves(x):
    hi = x.astype(bf16)
    return hi, (x - hi.astype(f32)).astype(bf16)


def fold(v, ref):
    whole = ref.shape[1]
    rest = v.shape[1] - whole
    each = 12 * 128 // whole
    parts = []
    for g in range(12):
        parts.append(v[8 * g : 8 * (g + 1), whole:])
        if (g + 1) % each == 0:
            parts.append(jnp.zeros((8, 128 - each * rest), f32))
    ref[:ROWS] = v[:, :whole]
    ref[ROWS:] = jnp.concatenate(parts, axis=1)


def unfold(ref, rest):
    each = 12 * 128 // ref.shape[1]
    starts = [128 * (g // each) + rest * (g % each) for g in range(12)]
    last = jnp.concatenate([ref[ROWS : ROWS + 8, a : a + rest] for a in starts], axis=0)
    return jnp.concatenate([ref[:ROWS], last], axis=1)


def pack_kernel(q, blocks_ref, down_ref, up_ref, own_ref, held, sems):
    cuts = (0, 6, 12, 18, F)
    copies = []
    for n in range(4):
        f = pl.ds(cuts[n], cuts[n + 1] - cuts[n])
        copies.append(pltpu.make_async_copy(blocks_ref.at[q, f], held.at[f], sems.at[n]))
    for copy in copies:
        copy.start()
    for copy in copies:
        copy.wait()
    parts = [held[f] for f in range(F)] + [jnp.zeros((MT, WIDE), f32)]
    own = jnp.concatenate(parts, axis=0)
    own_ref[:, :WIDE] = own
    own_ref[:, WIDE:] = jnp.zeros((ROWS, LANES - WIDE), f32)
    down_ref[...] = own[:, :EDGE]
    up_ref[...] = jnp.concatenate([own[:, 276:], blank(EDGE - 552)], axis=1)


def blank(width):
    return jnp.zeros((ROWS, width), f32)


def side_kernel(odd_ref, margin_ref, ham_ref, cross_ref):
    def packed(o):
        parts = [ref[:, 276 * n + o : 276 * n + o + 184] for ref in (margin_ref, ham_ref) for n in range(3)]
        return jnp.concatenate(parts + [blank(SIDE - 6 * 184)], axis=1)

    cross_ref[...] = jnp.where(odd_ref[0] == 1, packed(TILE), packed(0))


def corner_kernel(odd_ref, own_ref, plus_ref, minus_ref, cross_ref, inner_ref, near_ref):
    rows = (plus_ref[:, :552], minus_ref[:, :552])
    own = own_ref[...]

    def packed(o):
        parts = [v[:, 276 * n + o : 276 * n + o + 184] for v in rows for n in range(2)]
        return jnp.concatenate(parts + [blank(CORNER - 184 * 4)], axis=1)

    def near(o):
        parts = [own[:, 276 * n + o : 276 * n + o + 184] for n in range(3)]
        return jnp.concatenate(parts + [blank(NEAR - 184 * 3)], axis=1)

    odd = odd_ref[0] == 1
    to_plus, to_minus = packed(TILE), packed(0)
    cross_ref[...] = jnp.where(odd, to_plus, to_minus)
    inner_ref[...] = jnp.where(odd, to_minus, to_plus)
    near_ref[...] = jnp.where(odd, near(0), near(TILE))


def put(block, at, hi_ref, lo_ref):
    hi = block.astype(bf16)
    hi_ref[at] = hi
    lo_ref[at] = (block - hi.astype(f32)).astype(bf16)


def diagonal(rows, shift):
    row = lax.broadcasted_iota(jnp.int32, (rows, B), 0)
    return row == lax.broadcasted_iota(jnp.int32, (rows, B), 1) + shift


def part(i):
    return slice(B * i, B * (i + 1))


def column_sums(matrix):
    return jnp.sum(jnp.abs(matrix), axis=0, keepdims=True)


def largest(sums):
    return jnp.max(jnp.maximum(jnp.maximum(sums[0], sums[1]), sums[2]))


def assemble(q, odd_ref, codes_ref, own_ref, plus_ref, minus_ref, side_ref, cross_ref, inner_ref, near_ref, work, unit, sink):
    rows, picked, cols = work

    def set_rows(t, v):
        for c in range(LANES // 128):
            rows[c, t * ROWS : (t + 1) * ROWS] = v[:, 128 * c : 128 * (c + 1)]

    set_rows(4, own_ref[...])
    set_rows(7, jnp.concatenate([blank(276), plus_ref[:, :552], blank(LANES - 828)], axis=1))
    set_rows(1, jnp.concatenate([minus_ref[:, :552], blank(LANES - 552)], axis=1))
    set_rows(9, blank(LANES))

    def place(side_ref, begin, corner_ref, ahead):
        gap = TILE * ahead
        for base, ref, first, count, left in (
            (3, side_ref, begin, 3, 0), (6, corner_ref, 0, 2, 276), (0, corner_ref, 368, 2, 0),
        ):
            parts = [blank(left + gap)] if left + gap else []
            for n in range(count):
                parts += [ref[:, first + 184 * n : first + 184 * (n + 1)], blank(TILE)]
            parts[-1] = blank(LANES - left - gap - 276 * count + TILE)
            set_rows(base + 2 * ahead, jnp.concatenate(parts, axis=1))

    @pl.when(odd_ref[0] == 1)
    def _():
        place(side_ref, 552 * q, cross_ref, 1)
        place(near_ref, 0, inner_ref, 0)

    @pl.when(odd_ref[0] != 1)
    def _():
        place(side_ref, 552 * q, cross_ref, 0)
        place(near_ref, 0, inner_ref, 1)

    codes = [codes_ref[k] for k in range(SUBMOL)]
    begin = [jnp.where(c >= 0, (c >> 2) * ROWS + (c & 3), 9 * ROWS) for c in codes]
    for c in range(LANES // 128):
        for h in range(2):
            slots = range(16 * h, 16 * (h + 1))
            turned = jnp.concatenate([rows[c, pl.ds(begin[k], G, stride=MT)] for k in slots], axis=0).T
            for j in range(3):
                cols[3 * h + j, 128 * c : 128 * (c + 1)] = turned[:, 128 * j : 128 * (j + 1)]
    begin = [jnp.where(c >= 0, c * F, ZERO) for c in codes]
    row = lax.broadcasted_iota(jnp.int32, (8, 128), 0)
    lane = lax.broadcasted_iota(jnp.int32, (G, 128), 1)
    line = lax.broadcasted_iota(jnp.int32, (G, 128), 0)
    for k in range(SUBMOL):
        for j in range(DIM // 128):
            block = cols[j, pl.ds(begin[k], G)]
            block = jnp.concatenate([block[:16], jnp.where(row < 7, block[16:], 0.0)], axis=0)
            if unit and G * k < 128 * (j + 1) and G * (k + 1) > 128 * j:
                ones = jnp.where(lane + 128 * j == line + G * k, 1.0, 0.0)
                block = jnp.where(codes[k] >= 0, block, ones)
            picked[k * G : (k + 1) * G, 128 * j : 128 * (j + 1)] = block
    for i in range(3):
        for j in range(i, 3):
            sink(i, j, 0.5 * (picked[part(i), part(j)] + picked[part(j), part(i)].T))


def symmetric_product(ah, al, bh, bl, sink):
    for j in range(3):
        c = part(j)
        r = B * (j + 1)
        block = dot(ah[:r], bh[:, c]) + dot(ah[:r], bl[:, c]) + dot(al[:r], bh[:, c])
        for i in range(j + 1):
            sink(i, j, block[part(i)])


def symmetric_square(h, l, mixed, sink):
    for j in range(3):
        c = part(j)
        mixed[:, c] = dot(h[...], l[:, c])
        square = dot(h[: B * (j + 1)], h[:, c])
        for i in range(j + 1):
            sink(i, j, square[part(i)] + (mixed[part(i), c] + mixed[c, part(i)].T))


def put_both(i, j, block, hi_ref, lo_ref):
    put(block, (part(i), part(j)), hi_ref, lo_ref)
    if i < j:
        put(block.T, (part(j), part(i)), hi_ref, lo_ref)


def root_kernel(
    odd_ref, codes_ref, own_ref, plus_ref, minus_ref, side_ref, cross_ref, inner_ref, near_ref,
    margin_ref, root_hi, root_lo, rows, picked, cols, hi, lo, hi2, lo2,
):
    sums = [jnp.zeros((1, B), f32)] * 3

    def first(i, j, block):
        margin_ref[part(i), part(j)] = block
        put_both(i, j, block, hi, lo)
        sums[j] += column_sums(block)
        if i < j:
            other = block.T
            margin_ref[part(j), part(i)] = other
            sums[i] += column_sums(other)

    assemble(
        0, odd_ref, codes_ref, own_ref, plus_ref, minus_ref, side_ref, cross_ref, inner_ref, near_ref,
        (rows, picked, cols), True, first,
    )
    bound = largest(sums)
    one = 1.0 / jnp.full((1, B), bound, f32)
    two = one * one
    root = lax.rsqrt(jnp.full((1, B), bound, f32)) * 0.0625

    def second(i, j, block):
        value = block * two - (4.5 * one) * margin_ref[part(i), part(j)]
        if i == j:
            value = value + jnp.where(diagonal(B, 0), 3.375, 0.0)
        put_both(i, j, value, hi2, lo2)

    symmetric_square(hi, lo, picked, second)

    def third(i, j, block):
        value = block - (8.625 * one) * margin_ref[part(i), part(j)]
        if i == j:
            value = value + jnp.where(diagonal(B, 0), 24.609375, 0.0)
        put_both(i, j, value * root, root_hi, root_lo)

    symmetric_square(hi2, lo2, picked, third)


def density_kernel(
    odd_ref, codes_ref, chem_ref, own_ref, plus_ref, minus_ref, side_ref, cross_ref, inner_ref, near_ref,
    margin_ref, root_hi, root_lo, spread, up_ref, mid_ref, down_ref,
    rows, picked, cols, hi, lo, hi2, lo2, hi3, lo3, narrow, tall, pieces,
):
    chem = chem_ref[0]

    def first(i, j, block):
        put_both(i, j, block - chem * margin_ref[part(i), part(j)], hi, lo)

    assemble(
        1, odd_ref, codes_ref, own_ref, plus_ref, minus_ref, side_ref, cross_ref, inner_ref, near_ref,
        (rows, picked, cols), False, first,
    )
    for j in range(3):
        c = part(j)
        half = dot(root_hi[...], hi[:, c]) + dot(root_hi[...], lo[:, c]) + dot(root_lo[...], hi[:, c])
        put(half, (slice(None), c), hi2, lo2)
    sums = [jnp.zeros((1, B), f32)] * 3

    def second(i, j, block):
        put(block, (part(i), part(j)), hi, lo)
        sums[j] += column_sums(block)
        if i < j:
            other = block.T
            put(other, (part(j), part(i)), hi, lo)
            sums[i] += column_sums(other)

    symmetric_product(hi2, lo2, root_hi, root_lo, second)
    scale = 1.0 / jnp.full((1, B), largest(sums) + 1e-06, f32)
    half_two = 0.5 * (scale * scale)

    def third(i, j, block):
        value = -half_two * block
        if i == j:
            value = value + jnp.where(diagonal(B, 0), 1.5, 0.0)
        put_both(i, j, value, hi2, lo2)

    symmetric_square(hi, lo, picked, third)

    def fourth(i, j, block):
        put_both(i, j, block * scale, hi3, lo3)

    symmetric_product(hi, lo, hi2, lo2, fourth)

    def thin(v, bh, bl):
        vh, vl = halves(v)
        both = jnp.concatenate([vh, vl], axis=0)
        whole = dot(both, bh[...])
        return whole[:ROWS] + whole[ROWS:] + dot(vh, bl[...])

    def fifth(i, j, block):
        put_both(i, j, block, hi2, lo2)

    symmetric_square(hi3, lo3, picked, fifth)

    def squared(v):
        return thin(v, hi2, lo2)

    def factor(v):
        return 1.5 * v - 0.5 * squared(v)

    core = root_hi[:ROWS].astype(f32) + root_lo[:ROWS].astype(f32)
    inside = factor(thin(core, hi3, lo3))
    last = 1.5 * inside - 0.5 * squared(factor(factor(inside)))
    density = thin(core - last, root_hi, root_lo)

    narrow[...] = jnp.zeros((128, DIM), f32)
    for m in range(MT):
        narrow[m * F : (m + 1) * F] = density[m * G : m * G + F]
    for j in range(DIM // 128):
        tall[128 * j : 128 * (j + 1)] = narrow[:, 128 * j : 128 * (j + 1)].T
    spread[...] = jnp.zeros((CODES * G, 128), f32)
    for k in range(SUBMOL):
        code = codes_ref[k]

        @pl.when(code >= 0)
        def _():
            spread[pl.ds(pl.multiple_of(code * G, 8), G)] = tall[k * G : (k + 1) * G]

    odd = odd_ref[0]
    for dx, ref in ((-1, down_ref), (0, mid_ref), (1, up_ref)):
        for dy in (-1, 0, 1):
            place = 1 + dy - 2 * dy * odd
            t = 3 * (dx + 1) + dy + 1
            for m in range(MT):
                block = spread[t * ROWS + m * G : t * ROWS + m * G + F]
                pieces[place, pl.ds(m, F, stride=MT)] = block
            pieces[place, MT * F :] = jnp.zeros((ROWS - MT * F, 128), f32)
        v = jnp.concatenate([pieces[n][:, :TILE] for n in range(3)], axis=1)
        if dx:
            fold(v, ref)
        else:
            ref[...] = v


def own_kernel(spread, w_ref, flat):
    for c in range(CODES):
        flat[c * F : c * F + G] = spread[c * G : (c + 1) * G]
    flat[WIDE:LANES] = jnp.zeros((LANES - WIDE, 128), f32)
    for c in range(LANES // 128):
        own = flat[128 * c : 128 * (c + 1)].T
        for m in range(MT):
            w_ref[c, pl.ds(m, F, stride=MT)] = own[m * F : (m + 1) * F]
        w_ref[c, MT * F :] = jnp.zeros((ROWS - MT * F, 128), f32)


def turn_kernel(mid_ref, up_ref, down_ref, cross_ref, inner_ref):
    rows = (mid_ref[...], unfold(up_ref, 20), unfold(down_ref, 20))
    fold(jnp.concatenate([v[:, :TILE] for v in rows], axis=1), cross_ref)
    fold(jnp.concatenate([v[:, 2 * TILE :] for v in rows], axis=1), inner_ref)


def final_kernel(odd_ref, w_ref, mid_ref, up_ref, down_ref, cross_ref, inner_ref, out_ref):
    odd = odd_ref[0] == 1
    cross, inner = unfold(cross_ref, 20), unfold(inner_ref, 20)
    plus = jnp.where(odd, cross, inner)
    minus = jnp.where(odd, inner, cross)
    middle = (mid_ref[...], unfold(up_ref, 20), unfold(down_ref, 20))
    parts = []
    for n in (1, 0, 2):
        parts += [v[:, TILE * k : TILE * (k + 1)] for v, k in ((minus, n), (middle[n], 1), (plus, n))]
    received = jnp.concatenate(parts, axis=1)
    own = jnp.concatenate([w_ref[c] for c in range(LANES // 128)], axis=1)
    whole = 0.5 * (own[: MT * F, :WIDE] + received[: MT * F])
    for g in range(F):
        out_ref[g] = whole[MT * g : MT * (g + 1)]


def struct(shape, dtype=f32):
    return jax.ShapeDtypeStruct(shape, dtype)


def shards(blocks, halo_members, chem_potential):
    n_x, n_y = lax.axis_size("gx"), lax.axis_size("gy")
    ahead = [(i, (i + 1) % n_x) for i in range(n_x)]
    back = [((i + 1) % n_x, i) for i in range(n_x)]
    crossing = [(j, (j + 1) % n_y if j % 2 else (j - 1) % n_y) for j in range(n_y)]
    inside = [(j, j ^ 1) for j in range(n_y)]
    odd = (lax.axis_index("gy") % 2).astype(jnp.int32).reshape(1)
    codes = jnp.concatenate([4 * MT + jnp.arange(MT, dtype=jnp.int32), halo_members[0, 0]])
    ANY = pl.BlockSpec(memory_space=pltpu.HBM)
    native = pltpu.with_memory_space_constraint(jnp.transpose(blocks[0, 0], (0, 2, 1, 3)), pltpu.HBM)

    plus, minus, own = [], [], []
    for q in range(2):
        down, up, mine = pl.pallas_call(
            functools.partial(pack_kernel, q),
            out_shape=[struct((ROWS, EDGE)), struct((ROWS, EDGE)), struct((ROWS, LANES))],
            in_specs=[ANY],
            out_specs=[VMEM] * 3,
            scratch_shapes=[pltpu.VMEM((F, MT, WIDE), f32), pltpu.SemaphoreType.DMA((4,))],
            name=f"pack{q}",
            compiler_params=params(),
        )(native)
        plus.append(lax.ppermute(down, "gx", back))
        minus.append(lax.ppermute(up, "gx", ahead))
        own.append(mine)
    side = pl.pallas_call(
        side_kernel,
        out_shape=struct((ROWS, SIDE)),
        in_specs=[SMEM, VMEM, VMEM],
        out_specs=VMEM,
        name="side",
        compiler_params=params(),
    )(odd, *own)
    side = lax.ppermute(side, "gy", crossing)
    corners = []
    for q in range(2):
        x, i, near = pl.pallas_call(
            corner_kernel,
            out_shape=[struct((ROWS, CORNER)), struct((ROWS, CORNER)), struct((ROWS, NEAR))],
            in_specs=[SMEM, VMEM, VMEM, VMEM],
            out_specs=[VMEM] * 3,
            name=f"corner{q}",
            compiler_params=params(),
            cost_estimate=pl.CostEstimate(flops=(0, 40000000000)[q], bytes_accessed=(1, 10**8)[q], transcendentals=0),
        )(odd, own[q], plus[q], minus[q])
        corners.append(
            (lax.ppermute(x, "gy", crossing), lax.ppermute(i, "gy", inside), lax.ppermute(near, "gy", inside))
        )
    square = pltpu.VMEM((DIM, DIM), bf16)
    work = [
        pltpu.VMEM((LANES // 128, 10 * ROWS, 128), f32),
        pltpu.VMEM((DIM, DIM), f32),
        pltpu.VMEM((DIM // 128, LANES, 128), f32),
    ]
    margin, root_hi, root_lo = pl.pallas_call(
        root_kernel,
        out_shape=[struct((DIM, DIM)), struct((DIM, DIM), bf16), struct((DIM, DIM), bf16)],
        in_specs=[SMEM, SMEM] + [VMEM] * 7,
        out_specs=[VMEM] * 3,
        scratch_shapes=work + [square] * 4,
        name="inverse_root",
        compiler_params=params(),
        cost_estimate=pl.CostEstimate(flops=4 * 2 * DIM**3, bytes_accessed=2**23, transcendentals=0),
    )(odd, codes, own[0], plus[0], minus[0], side, *corners[0])
    folded = struct((ROWS + 8, 256))
    spread, up, mid, down = pl.pallas_call(
        density_kernel,
        out_shape=[struct((CODES * G, 128)), folded, struct((ROWS, 3 * TILE)), folded],
        in_specs=[SMEM, SMEM, SMEM] + [VMEM] * 10,
        out_specs=[VMEM] * 4,
        scratch_shapes=work
        + [square] * 6
        + [pltpu.VMEM((128, DIM), f32), pltpu.VMEM((DIM, 128), f32), pltpu.VMEM((3, ROWS, 128), f32)],
        name="density",
        compiler_params=params(),
        cost_estimate=pl.CostEstimate(flops=12 * 2 * DIM**3, bytes_accessed=2**23, transcendentals=0),
    )(odd, codes, chem_potential, own[1], plus[1], minus[1], side, *corners[1], margin, root_hi, root_lo)
    from_minus = lax.ppermute(up, "gx", ahead)
    from_plus = lax.ppermute(down, "gx", back)
    w = pl.pallas_call(
        own_kernel,
        out_shape=struct((LANES // 128, ROWS, 128)),
        in_specs=[VMEM],
        out_specs=VMEM,
        scratch_shapes=[pltpu.VMEM((LANES, 128), f32)],
        name="own",
        compiler_params=params(),
    )(spread)
    x, i = pl.pallas_call(
        turn_kernel,
        out_shape=[folded] * 2,
        in_specs=[VMEM] * 3,
        out_specs=[VMEM] * 2,
        name="turn",
        compiler_params=params(),
    )(mid, from_minus, from_plus)
    x = lax.ppermute(x, "gy", crossing)
    i = lax.ppermute(i, "gy", inside)
    out = pl.pallas_call(
        final_kernel,
        out_shape=struct((F, MT, WIDE)),
        in_specs=[SMEM] + [VMEM] * 6,
        out_specs=VMEM,
        name="symmetrize",
        compiler_params=params(),
    )(odd, w, mid, from_minus, from_plus, x, i)
    return jnp.transpose(out, (1, 0, 2))[None, None]


def solution(mesh):
    return jax.shard_map(
        shards,
        mesh=mesh,
        in_specs=(P("gx", "gy", None, None, None, None), P("gx", "gy", None), P()),
        out_specs=P("gx", "gy", None, None, None),
        check_vma=False,
    )
```

```python
import functools

import jax
import jax.numpy as jnp
from jax import lax
from jax.experimental import pallas as pl
from jax.experimental.pallas import tpu as pltpu
from jax.sharding import PartitionSpec as P

F = 23
G = 24
SUBMOL = 32
MT = 4
TILE = MT * F
DIM = SUBMOL * G
ROWS = MT * G
CODES = 9 * MT
WIDE = 9 * TILE
LANES = 896
EDGE = 640
SIDE = 1152
CORNER = 768
NEAR = 640
ZERO = 840
B = 256
f32 = jnp.float32
bf16 = jnp.bfloat16
VMEM = pl.BlockSpec(memory_space=pltpu.VMEM)
SMEM = pl.BlockSpec(memory_space=pltpu.SMEM)
LIMIT = 32 * 2**20


def params():
    return pltpu.CompilerParams(vmem_limit_bytes=LIMIT)


def dot(a, b):
    return jnp.dot(a, b, preferred_element_type=f32)


def halves(x):
    hi = x.astype(bf16)
    return hi, (x - hi.astype(f32)).astype(bf16)


def fold(v, ref):
    whole = ref.shape[1]
    rest = v.shape[1] - whole
    each = 12 * 128 // whole
    parts = []
    for g in range(12):
        parts.append(v[8 * g : 8 * (g + 1), whole:])
        if (g + 1) % each == 0:
            parts.append(jnp.zeros((8, 128 - each * rest), f32))
    ref[:ROWS] = v[:, :whole]
    ref[ROWS:] = jnp.concatenate(parts, axis=1)


def unfold(ref, rest):
    each = 12 * 128 // ref.shape[1]
    starts = [128 * (g // each) + rest * (g % each) for g in range(12)]
    last = jnp.concatenate([ref[ROWS : ROWS + 8, a : a + rest] for a in starts], axis=0)
    return jnp.concatenate([ref[:ROWS], last], axis=1)


def pack(held, down_ref, up_ref, own_ref):
    own = jnp.concatenate([held[f] for f in range(F)] + [jnp.zeros((MT, WIDE), f32)], axis=0)
    own_ref[:, :WIDE] = own
    own_ref[:, WIDE:] = jnp.zeros((ROWS, LANES - WIDE), f32)
    down_ref[...] = own[:, :EDGE]
    up_ref[...] = jnp.concatenate([own[:, 276:], blank(EDGE - 552)], axis=1)


def margin_pack_kernel(blocks_ref, down_ref, up_ref, own_ref, ham_ref, held, sems):
    first = pltpu.make_async_copy(blocks_ref.at[0], held, sems.at[0])
    second = pltpu.make_async_copy(blocks_ref.at[1], ham_ref, sems.at[1])
    first.start()
    second.start()
    first.wait()
    pack(held, down_ref, up_ref, own_ref)
    second.wait()


def blank(width):
    return jnp.zeros((ROWS, width), f32)


def side_kernel(odd_ref, margin_ref, ham_ref, cross_ref):
    def packed(o):
        parts = [ref[:, 276 * n + o : 276 * n + o + 184] for ref in (margin_ref, ham_ref) for n in range(3)]
        return jnp.concatenate(parts + [blank(SIDE - 6 * 184)], axis=1)

    cross_ref[...] = jnp.where(odd_ref[0] == 1, packed(TILE), packed(0))


def corner_kernel(odd_ref, own_ref, plus_ref, minus_ref, cross_ref, inner_ref, near_ref):
    rows = (plus_ref[:, :552], minus_ref[:, :552])
    own = own_ref[...]

    def packed(o):
        parts = [v[:, 276 * n + o : 276 * n + o + 184] for v in rows for n in range(2)]
        return jnp.concatenate(parts + [blank(CORNER - 184 * 4)], axis=1)

    def near(o):
        parts = [own[:, 276 * n + o : 276 * n + o + 184] for n in range(3)]
        return jnp.concatenate(parts + [blank(NEAR - 184 * 3)], axis=1)

    odd = odd_ref[0] == 1
    to_plus, to_minus = packed(TILE), packed(0)
    cross_ref[...] = jnp.where(odd, to_plus, to_minus)
    inner_ref[...] = jnp.where(odd, to_minus, to_plus)
    near_ref[...] = jnp.where(odd, near(0), near(TILE))


def put(block, at, hi_ref, lo_ref):
    hi = block.astype(bf16)
    hi_ref[at] = hi
    lo_ref[at] = (block - hi.astype(f32)).astype(bf16)


def diagonal(rows, shift):
    row = lax.broadcasted_iota(jnp.int32, (rows, B), 0)
    return row == lax.broadcasted_iota(jnp.int32, (rows, B), 1) + shift


def part(i):
    return slice(B * i, B * (i + 1))


def column_sums(matrix):
    return jnp.sum(jnp.abs(matrix), axis=0, keepdims=True)


def largest(sums):
    return jnp.max(jnp.maximum(jnp.maximum(sums[0], sums[1]), sums[2]))


def assemble(q, odd_ref, codes_ref, own_ref, plus_ref, minus_ref, side_ref, cross_ref, inner_ref, near_ref, work, unit, sink):
    rows, picked, cols = work

    def set_rows(t, v):
        for c in range(LANES // 128):
            rows[c, t * ROWS : (t + 1) * ROWS] = v[:, 128 * c : 128 * (c + 1)]

    set_rows(4, own_ref[...])
    set_rows(7, jnp.concatenate([blank(276), plus_ref[:, :552], blank(LANES - 828)], axis=1))
    set_rows(1, jnp.concatenate([minus_ref[:, :552], blank(LANES - 552)], axis=1))
    set_rows(9, blank(LANES))

    def place(side_ref, begin, corner_ref, ahead):
        gap = TILE * ahead
        for base, ref, first, count, left in (
            (3, side_ref, begin, 3, 0), (6, corner_ref, 0, 2, 276), (0, corner_ref, 368, 2, 0),
        ):
            parts = [blank(left + gap)] if left + gap else []
            for n in range(count):
                parts += [ref[:, first + 184 * n : first + 184 * (n + 1)], blank(TILE)]
            parts[-1] = blank(LANES - left - gap - 276 * count + TILE)
            set_rows(base + 2 * ahead, jnp.concatenate(parts, axis=1))

    @pl.when(odd_ref[0] == 1)
    def _():
        place(side_ref, 552 * q, cross_ref, 1)
        place(near_ref, 0, inner_ref, 0)

    @pl.when(odd_ref[0] != 1)
    def _():
        place(side_ref, 552 * q, cross_ref, 0)
        place(near_ref, 0, inner_ref, 1)

    codes = [codes_ref[k] for k in range(SUBMOL)]
    begin = [jnp.where(c >= 0, (c >> 2) * ROWS + (c & 3), 9 * ROWS) for c in codes]
    for c in range(LANES // 128):
        for h in range(2):
            slots = range(16 * h, 16 * (h + 1))
            turned = jnp.concatenate([rows[c, pl.ds(begin[k], G, stride=MT)] for k in slots], axis=0).T
            for j in range(3):
                cols[3 * h + j, 128 * c : 128 * (c + 1)] = turned[:, 128 * j : 128 * (j + 1)]
    begin = [jnp.where(c >= 0, c * F, ZERO) for c in codes]
    row = lax.broadcasted_iota(jnp.int32, (8, 128), 0)
    lane = lax.broadcasted_iota(jnp.int32, (G, 128), 1)
    line = lax.broadcasted_iota(jnp.int32, (G, 128), 0)
    for k in range(SUBMOL):
        for j in range(DIM // 128):
            block = cols[j, pl.ds(begin[k], G)]
            block = jnp.concatenate([block[:16], jnp.where(row < 7, block[16:], 0.0)], axis=0)
            if unit and G * k < 128 * (j + 1) and G * (k + 1) > 128 * j:
                ones = jnp.where(lane + 128 * j == line + G * k, 1.0, 0.0)
                block = jnp.where(codes[k] >= 0, block, ones)
            picked[k * G : (k + 1) * G, 128 * j : 128 * (j + 1)] = block
    for i in range(3):
        for j in range(i, 3):
            sink(i, j, 0.5 * (picked[part(i), part(j)] + picked[part(j), part(i)].T))


def symmetric_product(ah, al, bh, bl, sink):
    for j in range(3):
        c = part(j)
        r = B * (j + 1)
        block = dot(ah[:r], bh[:, c]) + dot(ah[:r], bl[:, c]) + dot(al[:r], bh[:, c])
        for i in range(j + 1):
            sink(i, j, block[part(i)])


def symmetric_square(h, l, mixed, sink):
    for j in range(3):
        c = part(j)
        mixed[:, c] = dot(h[...], l[:, c])
        square = dot(h[: B * (j + 1)], h[:, c])
        for i in range(j + 1):
            sink(i, j, square[part(i)] + (mixed[part(i), c] + mixed[c, part(i)].T))


def put_both(i, j, block, hi_ref, lo_ref):
    put(block, (part(i), part(j)), hi_ref, lo_ref)
    if i < j:
        put(block.T, (part(j), part(i)), hi_ref, lo_ref)


def root_kernel(
    odd_ref, codes_ref, own_ref, plus_ref, minus_ref, side_ref, cross_ref, inner_ref, near_ref,
    margin_ref, root_hi, root_lo, rows, picked, cols, hi, lo, hi2, lo2,
):
    sums = [jnp.zeros((1, B), f32)] * 3

    def first(i, j, block):
        margin_ref[part(i), part(j)] = block
        put_both(i, j, block, hi, lo)
        sums[j] += column_sums(block)
        if i < j:
            other = block.T
            margin_ref[part(j), part(i)] = other
            sums[i] += column_sums(other)

    assemble(
        0, odd_ref, codes_ref, own_ref, plus_ref, minus_ref, side_ref, cross_ref, inner_ref, near_ref,
        (rows, picked, cols), True, first,
    )
    bound = largest(sums)
    one = 1.0 / jnp.full((1, B), bound, f32)
    two = one * one
    root = lax.rsqrt(jnp.full((1, B), bound, f32)) * 0.0625

    def second(i, j, block):
        value = block * two - (4.5 * one) * margin_ref[part(i), part(j)]
        if i == j:
            value = value + jnp.where(diagonal(B, 0), 3.375, 0.0)
        put_both(i, j, value, hi2, lo2)

    symmetric_square(hi, lo, picked, second)

    def third(i, j, block):
        value = block - (8.625 * one) * margin_ref[part(i), part(j)]
        if i == j:
            value = value + jnp.where(diagonal(B, 0), 24.609375, 0.0)
        put_both(i, j, value * root, root_hi, root_lo)

    symmetric_square(hi2, lo2, picked, third)


def density_kernel(
    odd_ref, codes_ref, chem_ref, own_ref, plus_ref, minus_ref, side_ref, cross_ref, inner_ref, near_ref,
    margin_ref, root_hi, root_lo, spread, up_ref, mid_ref, down_ref,
    rows, picked, cols, hi, lo, hi2, lo2, hi3, lo3, narrow, tall, pieces,
):
    chem = chem_ref[0]

    def first(i, j, block):
        put_both(i, j, block - chem * margin_ref[part(i), part(j)], hi, lo)

    assemble(
        1, odd_ref, codes_ref, own_ref, plus_ref, minus_ref, side_ref, cross_ref, inner_ref, near_ref,
        (rows, picked, cols), False, first,
    )
    for j in range(3):
        c = part(j)
        half = dot(root_hi[...], hi[:, c]) + dot(root_hi[...], lo[:, c]) + dot(root_lo[...], hi[:, c])
        put(half, (slice(None), c), hi2, lo2)
    sums = [jnp.zeros((1, B), f32)] * 3

    def second(i, j, block):
        put(block, (part(i), part(j)), hi, lo)
        sums[j] += column_sums(block)
        if i < j:
            other = block.T
            put(other, (part(j), part(i)), hi, lo)
            sums[i] += column_sums(other)

    symmetric_product(hi2, lo2, root_hi, root_lo, second)
    scale = 1.0 / jnp.full((1, B), largest(sums) + 1e-06, f32)
    half_two = 0.5 * (scale * scale)

    def third(i, j, block):
        value = -half_two * block
        if i == j:
            value = value + jnp.where(diagonal(B, 0), 1.5, 0.0)
        put_both(i, j, value, hi2, lo2)

    symmetric_square(hi, lo, picked, third)

    def fourth(i, j, block):
        put_both(i, j, block * scale, hi3, lo3)

    symmetric_product(hi, lo, hi2, lo2, fourth)

    def thin(v, bh, bl):
        vh, vl = halves(v)
        both = jnp.concatenate([vh, vl], axis=0)
        whole = dot(both, bh[...])
        return whole[:ROWS] + whole[ROWS:] + dot(vh, bl[...])

    def fifth(i, j, block):
        put_both(i, j, block, hi2, lo2)

    symmetric_square(hi3, lo3, picked, fifth)

    def squared(v):
        return thin(v, hi2, lo2)

    def factor(v):
        return 1.5 * v - 0.5 * squared(v)

    core = root_hi[:ROWS].astype(f32) + root_lo[:ROWS].astype(f32)
    inside = factor(thin(core, hi3, lo3))
    last = 1.5 * inside - 0.5 * squared(factor(factor(inside)))
    density = thin(core - last, root_hi, root_lo)

    narrow[...] = jnp.zeros((128, DIM), f32)
    for m in range(MT):
        narrow[m * F : (m + 1) * F] = density[m * G : m * G + F]
    for j in range(DIM // 128):
        tall[128 * j : 128 * (j + 1)] = narrow[:, 128 * j : 128 * (j + 1)].T
    spread[...] = jnp.zeros((CODES * G, 128), f32)
    for k in range(SUBMOL):
        code = codes_ref[k]

        @pl.when(code >= 0)
        def _():
            spread[pl.ds(pl.multiple_of(code * G, 8), G)] = tall[k * G : (k + 1) * G]

    odd = odd_ref[0]
    for dx, ref in ((-1, down_ref), (0, mid_ref), (1, up_ref)):
        for dy in (-1, 0, 1):
            place = 1 + dy - 2 * dy * odd
            t = 3 * (dx + 1) + dy + 1
            for m in range(MT):
                block = spread[t * ROWS + m * G : t * ROWS + m * G + F]
                pieces[place, pl.ds(m, F, stride=MT)] = block
            pieces[place, MT * F :] = jnp.zeros((ROWS - MT * F, 128), f32)
        v = jnp.concatenate([pieces[n][:, :TILE] for n in range(3)], axis=1)
        if dx:
            fold(v, ref)
        else:
            ref[...] = v


def own_kernel(spread, w_ref, flat):
    for c in range(CODES):
        flat[c * F : c * F + G] = spread[c * G : (c + 1) * G]
    flat[WIDE:LANES] = jnp.zeros((LANES - WIDE, 128), f32)
    for c in range(LANES // 128):
        own = flat[128 * c : 128 * (c + 1)].T
        for m in range(MT):
            w_ref[c, pl.ds(m, F, stride=MT)] = own[m * F : (m + 1) * F]
        w_ref[c, MT * F :] = jnp.zeros((ROWS - MT * F, 128), f32)


def turn_kernel(mid_ref, up_ref, down_ref, cross_ref, inner_ref):
    rows = (mid_ref[...], unfold(up_ref, 20), unfold(down_ref, 20))
    fold(jnp.concatenate([v[:, :TILE] for v in rows], axis=1), cross_ref)
    fold(jnp.concatenate([v[:, 2 * TILE :] for v in rows], axis=1), inner_ref)


def final_kernel(odd_ref, w_ref, mid_ref, up_ref, down_ref, cross_ref, inner_ref, out_ref):
    odd = odd_ref[0] == 1
    cross, inner = unfold(cross_ref, 20), unfold(inner_ref, 20)
    plus = jnp.where(odd, cross, inner)
    minus = jnp.where(odd, inner, cross)
    middle = (mid_ref[...], unfold(up_ref, 20), unfold(down_ref, 20))
    parts = []
    for n in (1, 0, 2):
        parts += [v[:, TILE * k : TILE * (k + 1)] for v, k in ((minus, n), (middle[n], 1), (plus, n))]
    received = jnp.concatenate(parts, axis=1)
    own = jnp.concatenate([w_ref[c] for c in range(LANES // 128)], axis=1)
    whole = 0.5 * (own[: MT * F, :WIDE] + received[: MT * F])
    for g in range(F):
        out_ref[g] = whole[MT * g : MT * (g + 1)]


def struct(shape, dtype=f32):
    return jax.ShapeDtypeStruct(shape, dtype)


def shards(blocks, halo_members, chem_potential):
    n_x, n_y = lax.axis_size("gx"), lax.axis_size("gy")
    ahead = [(i, (i + 1) % n_x) for i in range(n_x)]
    back = [((i + 1) % n_x, i) for i in range(n_x)]
    crossing = [(j, (j + 1) % n_y if j % 2 else (j - 1) % n_y) for j in range(n_y)]
    inside = [(j, j ^ 1) for j in range(n_y)]
    odd = (lax.axis_index("gy") % 2).astype(jnp.int32).reshape(1)
    codes = jnp.concatenate([4 * MT + jnp.arange(MT, dtype=jnp.int32), halo_members[0, 0]])
    ANY = pl.BlockSpec(memory_space=pltpu.HBM)
    native = pltpu.with_memory_space_constraint(jnp.transpose(blocks[0, 0], (0, 2, 1, 3)), pltpu.HBM)

    plus, minus, own = [], [], []
    packed = [struct((ROWS, EDGE)), struct((ROWS, EDGE)), struct((ROWS, LANES))]
    down, up, mine, ham = pl.pallas_call(
        margin_pack_kernel,
        out_shape=packed + [struct((F, MT, WIDE))],
        in_specs=[ANY],
        out_specs=[VMEM] * 4,
        scratch_shapes=[pltpu.VMEM((F, MT, WIDE), f32), pltpu.SemaphoreType.DMA((2,))],
        name="pack0",
        compiler_params=params(),
    )(native)
    for q in range(2):
        if q:
            down, up, mine = pl.pallas_call(
                pack,
                out_shape=packed,
                in_specs=[VMEM],
                out_specs=[VMEM] * 3,
                name="pack1",
                compiler_params=params(),
                cost_estimate=pl.CostEstimate(flops=10**6, bytes_accessed=10**6, transcendentals=0),
            )(ham)
        plus.append(lax.ppermute(down, "gx", back))
        minus.append(lax.ppermute(up, "gx", ahead))
        own.append(mine)
    side = pl.pallas_call(
        side_kernel,
        out_shape=struct((ROWS, SIDE)),
        in_specs=[SMEM, VMEM, VMEM],
        out_specs=VMEM,
        name="side",
        compiler_params=params(),
    )(odd, *own)
    side = lax.ppermute(side, "gy", crossing)
    corners = []
    for q in range(2):
        x, i, near = pl.pallas_call(
            corner_kernel,
            out_shape=[struct((ROWS, CORNER)), struct((ROWS, CORNER)), struct((ROWS, NEAR))],
            in_specs=[SMEM, VMEM, VMEM, VMEM],
            out_specs=[VMEM] * 3,
            name=f"corner{q}",
            compiler_params=params(),
            cost_estimate=pl.CostEstimate(flops=(0, 40000000000)[q], bytes_accessed=(1, 10**8)[q], transcendentals=0),
        )(odd, own[q], plus[q], minus[q])
        corners.append(
            (lax.ppermute(x, "gy", crossing), lax.ppermute(i, "gy", inside), lax.ppermute(near, "gy", inside))
        )
    square = pltpu.VMEM((DIM, DIM), bf16)
    work = [
        pltpu.VMEM((LANES // 128, 10 * ROWS, 128), f32),
        pltpu.VMEM((DIM, DIM), f32),
        pltpu.VMEM((DIM // 128, LANES, 128), f32),
    ]
    margin, root_hi, root_lo = pl.pallas_call(
        root_kernel,
        out_shape=[struct((DIM, DIM)), struct((DIM, DIM), bf16), struct((DIM, DIM), bf16)],
        in_specs=[SMEM, SMEM] + [VMEM] * 7,
        out_specs=[VMEM] * 3,
        scratch_shapes=work + [square] * 4,
        name="inverse_root",
        compiler_params=params(),
        cost_estimate=pl.CostEstimate(flops=4 * 2 * DIM**3, bytes_accessed=2**23, transcendentals=0),
    )(odd, codes, own[0], plus[0], minus[0], side, *corners[0])
    folded = struct((ROWS + 8, 256))
    spread, up, mid, down = pl.pallas_call(
        density_kernel,
        out_shape=[struct((CODES * G, 128)), folded, struct((ROWS, 3 * TILE)), folded],
        in_specs=[SMEM, SMEM, SMEM] + [VMEM] * 10,
        out_specs=[VMEM] * 4,
        scratch_shapes=work
        + [square] * 6
        + [pltpu.VMEM((128, DIM), f32), pltpu.VMEM((DIM, 128), f32), pltpu.VMEM((3, ROWS, 128), f32)],
        name="density",
        compiler_params=params(),
        cost_estimate=pl.CostEstimate(flops=12 * 2 * DIM**3, bytes_accessed=2**23, transcendentals=0),
    )(odd, codes, chem_potential, own[1], plus[1], minus[1], side, *corners[1], margin, root_hi, root_lo)
    from_minus = lax.ppermute(up, "gx", ahead)
    from_plus = lax.ppermute(down, "gx", back)
    w = pl.pallas_call(
        own_kernel,
        out_shape=struct((LANES // 128, ROWS, 128)),
        in_specs=[VMEM],
        out_specs=VMEM,
        scratch_shapes=[pltpu.VMEM((LANES, 128), f32)],
        name="own",
        compiler_params=params(),
    )(spread)
    x, i = pl.pallas_call(
        turn_kernel,
        out_shape=[folded] * 2,
        in_specs=[VMEM] * 3,
        out_specs=[VMEM] * 2,
        name="turn",
        compiler_params=params(),
    )(mid, from_minus, from_plus)
    x = lax.ppermute(x, "gy", crossing)
    i = lax.ppermute(i, "gy", inside)
    out = pl.pallas_call(
        final_kernel,
        out_shape=struct((F, MT, WIDE)),
        in_specs=[SMEM] + [VMEM] * 6,
        out_specs=VMEM,
        name="symmetrize",
        compiler_params=params(),
    )(odd, w, mid, from_minus, from_plus, x, i)
    return jnp.transpose(out, (1, 0, 2))[None, None]


def solution(mesh):
    return jax.shard_map(
        shards,
        mesh=mesh,
        in_specs=(P("gx", "gy", None, None, None, None), P("gx", "gy", None), P()),
        out_specs=P("gx", "gy", None, None, None),
        check_vma=False,
    )
```

```python
import functools

import jax
import jax.numpy as jnp
from jax import lax
from jax.experimental import pallas as pl
from jax.experimental.pallas import tpu as pltpu
from jax.sharding import PartitionSpec as P

F = 23
G = 24
SUBMOL = 32
MT = 4
TILE = MT * F
DIM = SUBMOL * G
ROWS = MT * G
CODES = 9 * MT
WIDE = 9 * TILE
LANES = 896
EDGE = 640
SIDE = 1152
CORNER = 768
NEAR = 640
ZERO = 840
B = 256
f32 = jnp.float32
bf16 = jnp.bfloat16
VMEM = pl.BlockSpec(memory_space=pltpu.VMEM)
SMEM = pl.BlockSpec(memory_space=pltpu.SMEM)
LIMIT = 32 * 2**20


def params():
    return pltpu.CompilerParams(vmem_limit_bytes=LIMIT)


def dot(a, b):
    return jnp.dot(a, b, preferred_element_type=f32)


def halves(x):
    hi = x.astype(bf16)
    return hi, (x - hi.astype(f32)).astype(bf16)


def fold(v, ref):
    whole = ref.shape[1]
    rest = v.shape[1] - whole
    each = 12 * 128 // whole
    parts = []
    for g in range(12):
        parts.append(v[8 * g : 8 * (g + 1), whole:])
        if (g + 1) % each == 0:
            parts.append(jnp.zeros((8, 128 - each * rest), f32))
    ref[:ROWS] = v[:, :whole]
    ref[ROWS:] = jnp.concatenate(parts, axis=1)


def unfold(ref, rest):
    each = 12 * 128 // ref.shape[1]
    starts = [128 * (g // each) + rest * (g % each) for g in range(12)]
    last = jnp.concatenate([ref[ROWS : ROWS + 8, a : a + rest] for a in starts], axis=0)
    return jnp.concatenate([ref[:ROWS], last], axis=1)


def edge(ref):
    return unfold(ref, 40) if ref.shape[1] < EDGE else ref[:, :552]


def pack(held, down_ref, up_ref, own_ref):
    own = jnp.concatenate([held[f] for f in range(F)] + [jnp.zeros((MT, WIDE), f32)], axis=0)
    own_ref[:, :WIDE] = own
    own_ref[:, WIDE:] = jnp.zeros((ROWS, LANES - WIDE), f32)
    if down_ref.shape[1] < EDGE:
        fold(own[:, :552], down_ref)
        fold(own[:, 276:], up_ref)
    else:
        down_ref[...] = own[:, :EDGE]
        up_ref[...] = jnp.concatenate([own[:, 276:], blank(EDGE - 552)], axis=1)


def margin_pack_kernel(blocks_ref, down_ref, up_ref, own_ref, ham_ref, held, sems):
    first = pltpu.make_async_copy(blocks_ref.at[0], held, sems.at[0])
    second = pltpu.make_async_copy(blocks_ref.at[1], ham_ref, sems.at[1])
    first.start()
    second.start()
    first.wait()
    pack(held, down_ref, up_ref, own_ref)
    second.wait()


def blank(width):
    return jnp.zeros((ROWS, width), f32)


def side_kernel(odd_ref, margin_ref, ham_ref, cross_ref):
    def packed(o):
        parts = [ref[:, 276 * n + o : 276 * n + o + 184] for ref in (margin_ref, ham_ref) for n in range(3)]
        return jnp.concatenate(parts + [blank(SIDE - 6 * 184)], axis=1)

    cross_ref[...] = jnp.where(odd_ref[0] == 1, packed(TILE), packed(0))


def corner_kernel(odd_ref, own_ref, plus_ref, minus_ref, cross_ref, inner_ref, near_ref):
    rows = (edge(plus_ref), edge(minus_ref))
    own = own_ref[...]

    def packed(o):
        parts = [v[:, 276 * n + o : 276 * n + o + 184] for v in rows for n in range(2)]
        return jnp.concatenate(parts + [blank(CORNER - 184 * 4)], axis=1)

    def near(o):
        parts = [own[:, 276 * n + o : 276 * n + o + 184] for n in range(3)]
        return jnp.concatenate(parts + [blank(NEAR - 184 * 3)], axis=1)

    odd = odd_ref[0] == 1
    to_plus, to_minus = packed(TILE), packed(0)
    cross_ref[...] = jnp.where(odd, to_plus, to_minus)
    inner_ref[...] = jnp.where(odd, to_minus, to_plus)
    near_ref[...] = jnp.where(odd, near(0), near(TILE))


def put(block, at, hi_ref, lo_ref):
    hi = block.astype(bf16)
    hi_ref[at] = hi
    lo_ref[at] = (block - hi.astype(f32)).astype(bf16)


def diagonal(rows, shift):
    row = lax.broadcasted_iota(jnp.int32, (rows, B), 0)
    return row == lax.broadcasted_iota(jnp.int32, (rows, B), 1) + shift


def part(i):
    return slice(B * i, B * (i + 1))


def column_sums(matrix):
    return jnp.sum(jnp.abs(matrix), axis=0, keepdims=True)


def largest(sums):
    return jnp.max(jnp.maximum(jnp.maximum(sums[0], sums[1]), sums[2]))


def assemble(q, odd_ref, codes_ref, own_ref, plus_ref, minus_ref, side_ref, cross_ref, inner_ref, near_ref, work, unit, sink):
    rows, picked, cols = work

    def set_rows(t, v):
        for c in range(LANES // 128):
            rows[c, t * ROWS : (t + 1) * ROWS] = v[:, 128 * c : 128 * (c + 1)]

    set_rows(4, own_ref[...])
    set_rows(7, jnp.concatenate([blank(276), edge(plus_ref), blank(LANES - 828)], axis=1))
    set_rows(1, jnp.concatenate([edge(minus_ref), blank(LANES - 552)], axis=1))
    set_rows(9, blank(LANES))

    def place(side_ref, begin, corner_ref, ahead):
        gap = TILE * ahead
        for base, ref, first, count, left in (
            (3, side_ref, begin, 3, 0), (6, corner_ref, 0, 2, 276), (0, corner_ref, 368, 2, 0),
        ):
            parts = [blank(left + gap)] if left + gap else []
            for n in range(count):
                parts += [ref[:, first + 184 * n : first + 184 * (n + 1)], blank(TILE)]
            parts[-1] = blank(LANES - left - gap - 276 * count + TILE)
            set_rows(base + 2 * ahead, jnp.concatenate(parts, axis=1))

    @pl.when(odd_ref[0] == 1)
    def _():
        place(side_ref, 552 * q, cross_ref, 1)
        place(near_ref, 0, inner_ref, 0)

    @pl.when(odd_ref[0] != 1)
    def _():
        place(side_ref, 552 * q, cross_ref, 0)
        place(near_ref, 0, inner_ref, 1)

    codes = [codes_ref[k] for k in range(SUBMOL)]
    begin = [jnp.where(c >= 0, (c >> 2) * ROWS + (c & 3), 9 * ROWS) for c in codes]
    for c in range(LANES // 128):
        for h in range(2):
            slots = range(16 * h, 16 * (h + 1))
            turned = jnp.concatenate([rows[c, pl.ds(begin[k], G, stride=MT)] for k in slots], axis=0).T
            for j in range(3):
                cols[3 * h + j, 128 * c : 128 * (c + 1)] = turned[:, 128 * j : 128 * (j + 1)]
    begin = [jnp.where(c >= 0, c * F, ZERO) for c in codes]
    row = lax.broadcasted_iota(jnp.int32, (8, 128), 0)
    lane = lax.broadcasted_iota(jnp.int32, (G, 128), 1)
    line = lax.broadcasted_iota(jnp.int32, (G, 128), 0)
    for k in range(SUBMOL):
        for j in range(DIM // 128):
            block = cols[j, pl.ds(begin[k], G)]
            block = jnp.concatenate([block[:16], jnp.where(row < 7, block[16:], 0.0)], axis=0)
            if unit and G * k < 128 * (j + 1) and G * (k + 1) > 128 * j:
                ones = jnp.where(lane + 128 * j == line + G * k, 1.0, 0.0)
                block = jnp.where(codes[k] >= 0, block, ones)
            picked[k * G : (k + 1) * G, 128 * j : 128 * (j + 1)] = block
    for i in range(3):
        for j in range(i, 3):
            sink(i, j, 0.5 * (picked[part(i), part(j)] + picked[part(j), part(i)].T))


def symmetric_product(ah, al, bh, bl, sink):
    for j in range(3):
        c = part(j)
        r = B * (j + 1)
        block = dot(ah[:r], bh[:, c]) + dot(ah[:r], bl[:, c]) + dot(al[:r], bh[:, c])
        for i in range(j + 1):
            sink(i, j, block[part(i)])


def symmetric_square(h, l, mixed, sink):
    for j in range(3):
        c = part(j)
        mixed[:, c] = dot(h[...], l[:, c])
        square = dot(h[: B * (j + 1)], h[:, c])
        for i in range(j + 1):
            sink(i, j, square[part(i)] + (mixed[part(i), c] + mixed[c, part(i)].T))


def put_both(i, j, block, hi_ref, lo_ref):
    put(block, (part(i), part(j)), hi_ref, lo_ref)
    if i < j:
        put(block.T, (part(j), part(i)), hi_ref, lo_ref)


def root_kernel(
    odd_ref, codes_ref, own_ref, plus_ref, minus_ref, side_ref, cross_ref, inner_ref, near_ref,
    margin_ref, root_hi, root_lo, rows, picked, cols, hi, lo, hi2, lo2,
):
    sums = [jnp.zeros((1, B), f32)] * 3

    def first(i, j, block):
        margin_ref[part(i), part(j)] = block
        put_both(i, j, block, hi, lo)
        sums[j] += column_sums(block)
        if i < j:
            other = block.T
            margin_ref[part(j), part(i)] = other
            sums[i] += column_sums(other)

    assemble(
        0, odd_ref, codes_ref, own_ref, plus_ref, minus_ref, side_ref, cross_ref, inner_ref, near_ref,
        (rows, picked, cols), True, first,
    )
    bound = largest(sums)
    one = 1.0 / jnp.full((1, B), bound, f32)
    two = one * one
    root = lax.rsqrt(jnp.full((1, B), bound, f32)) * 0.0625

    def second(i, j, block):
        value = block * two - (4.5 * one) * margin_ref[part(i), part(j)]
        if i == j:
            value = value + jnp.where(diagonal(B, 0), 3.375, 0.0)
        put_both(i, j, value, hi2, lo2)

    symmetric_square(hi, lo, picked, second)

    def third(i, j, block):
        value = block - (8.625 * one) * margin_ref[part(i), part(j)]
        if i == j:
            value = value + jnp.where(diagonal(B, 0), 24.609375, 0.0)
        put_both(i, j, value * root, root_hi, root_lo)

    symmetric_square(hi2, lo2, picked, third)


def density_kernel(
    odd_ref, codes_ref, chem_ref, own_ref, plus_ref, minus_ref, side_ref, cross_ref, inner_ref, near_ref,
    margin_ref, root_hi, root_lo, spread, up_ref, mid_ref, down_ref,
    rows, picked, cols, hi, lo, hi2, lo2, hi3, lo3, narrow, tall, pieces,
):
    chem = chem_ref[0]

    def first(i, j, block):
        put_both(i, j, block - chem * margin_ref[part(i), part(j)], hi, lo)

    assemble(
        1, odd_ref, codes_ref, own_ref, plus_ref, minus_ref, side_ref, cross_ref, inner_ref, near_ref,
        (rows, picked, cols), False, first,
    )
    for j in range(3):
        c = part(j)
        half = dot(root_hi[...], hi[:, c]) + dot(root_hi[...], lo[:, c]) + dot(root_lo[...], hi[:, c])
        put(half, (slice(None), c), hi2, lo2)
    sums = [jnp.zeros((1, B), f32)] * 3

    def second(i, j, block):
        put(block, (part(i), part(j)), hi, lo)
        sums[j] += column_sums(block)
        if i < j:
            other = block.T
            put(other, (part(j), part(i)), hi, lo)
            sums[i] += column_sums(other)

    symmetric_product(hi2, lo2, root_hi, root_lo, second)
    scale = 1.0 / jnp.full((1, B), largest(sums) + 1e-06, f32)
    half_two = 0.5 * (scale * scale)

    def third(i, j, block):
        value = -half_two * block
        if i == j:
            value = value + jnp.where(diagonal(B, 0), 1.5, 0.0)
        put_both(i, j, value, hi2, lo2)

    symmetric_square(hi, lo, picked, third)

    def fourth(i, j, block):
        put_both(i, j, block * scale, hi3, lo3)

    symmetric_product(hi, lo, hi2, lo2, fourth)

    def thin(v, bh, bl):
        vh, vl = halves(v)
        both = jnp.concatenate([vh, vl], axis=0)
        whole = dot(both, bh[...])
        return whole[:ROWS] + whole[ROWS:] + dot(vh, bl[...])

    def fifth(i, j, block):
        put_both(i, j, block, hi2, lo2)

    symmetric_square(hi3, lo3, picked, fifth)

    def squared(v):
        return thin(v, hi2, lo2)

    def factor(v):
        return 1.5 * v - 0.5 * squared(v)

    core = root_hi[:ROWS].astype(f32) + root_lo[:ROWS].astype(f32)
    inside = factor(thin(core, hi3, lo3))
    last = 1.5 * inside - 0.5 * squared(factor(factor(inside)))
    density = thin(core - last, root_hi, root_lo)

    narrow[...] = jnp.zeros((128, DIM), f32)
    for m in range(MT):
        narrow[m * F : (m + 1) * F] = density[m * G : m * G + F]
    for j in range(DIM // 128):
        tall[128 * j : 128 * (j + 1)] = narrow[:, 128 * j : 128 * (j + 1)].T
    spread[...] = jnp.zeros((CODES * G, 128), f32)
    for k in range(SUBMOL):
        code = codes_ref[k]

        @pl.when(code >= 0)
        def _():
            spread[pl.ds(pl.multiple_of(code * G, 8), G)] = tall[k * G : (k + 1) * G]

    odd = odd_ref[0]
    for dx, ref in ((-1, down_ref), (0, mid_ref), (1, up_ref)):
        for dy in (-1, 0, 1):
            place = 1 + dy - 2 * dy * odd
            t = 3 * (dx + 1) + dy + 1
            for m in range(MT):
                block = spread[t * ROWS + m * G : t * ROWS + m * G + F]
                pieces[place, pl.ds(m, F, stride=MT)] = block
            pieces[place, MT * F :] = jnp.zeros((ROWS - MT * F, 128), f32)
        v = jnp.concatenate([pieces[n][:, :TILE] for n in range(3)], axis=1)
        if dx:
            fold(v, ref)
        else:
            ref[...] = v


def own_kernel(spread, w_ref, flat):
    for c in range(CODES):
        flat[c * F : c * F + G] = spread[c * G : (c + 1) * G]
    flat[WIDE:LANES] = jnp.zeros((LANES - WIDE, 128), f32)
    for c in range(LANES // 128):
        own = flat[128 * c : 128 * (c + 1)].T
        for m in range(MT):
            w_ref[c, pl.ds(m, F, stride=MT)] = own[m * F : (m + 1) * F]
        w_ref[c, MT * F :] = jnp.zeros((ROWS - MT * F, 128), f32)


def turn_kernel(mid_ref, up_ref, down_ref, cross_ref, inner_ref):
    rows = (mid_ref[...], unfold(up_ref, 20), unfold(down_ref, 20))
    fold(jnp.concatenate([v[:, :TILE] for v in rows], axis=1), cross_ref)
    fold(jnp.concatenate([v[:, 2 * TILE :] for v in rows], axis=1), inner_ref)


def final_kernel(odd_ref, w_ref, mid_ref, up_ref, down_ref, cross_ref, inner_ref, out_ref):
    odd = odd_ref[0] == 1
    cross, inner = unfold(cross_ref, 20), unfold(inner_ref, 20)
    plus = jnp.where(odd, cross, inner)
    minus = jnp.where(odd, inner, cross)
    middle = (mid_ref[...], unfold(up_ref, 20), unfold(down_ref, 20))
    parts = []
    for n in (1, 0, 2):
        parts += [v[:, TILE * k : TILE * (k + 1)] for v, k in ((minus, n), (middle[n], 1), (plus, n))]
    received = jnp.concatenate(parts, axis=1)
    own = jnp.concatenate([w_ref[c] for c in range(LANES // 128)], axis=1)
    whole = 0.5 * (own[: MT * F, :WIDE] + received[: MT * F])
    for g in range(F):
        out_ref[g] = whole[MT * g : MT * (g + 1)]


def struct(shape, dtype=f32):
    return jax.ShapeDtypeStruct(shape, dtype)


def shards(blocks, halo_members, chem_potential):
    n_x, n_y = lax.axis_size("gx"), lax.axis_size("gy")
    ahead = [(i, (i + 1) % n_x) for i in range(n_x)]
    back = [((i + 1) % n_x, i) for i in range(n_x)]
    crossing = [(j, (j + 1) % n_y if j % 2 else (j - 1) % n_y) for j in range(n_y)]
    inside = [(j, j ^ 1) for j in range(n_y)]
    odd = (lax.axis_index("gy") % 2).astype(jnp.int32).reshape(1)
    codes = jnp.concatenate([4 * MT + jnp.arange(MT, dtype=jnp.int32), halo_members[0, 0]])
    ANY = pl.BlockSpec(memory_space=pltpu.HBM)
    native = pltpu.with_memory_space_constraint(jnp.transpose(blocks[0, 0], (0, 2, 1, 3)), pltpu.HBM)

    plus, minus, own = [], [], []
    packed = [struct((ROWS, EDGE)), struct((ROWS, EDGE)), struct((ROWS, LANES))]
    down, up, mine, ham = pl.pallas_call(
        margin_pack_kernel,
        out_shape=[struct((ROWS + 8, 512)), struct((ROWS + 8, 512)), packed[2], struct((F, MT, WIDE))],
        in_specs=[ANY],
        out_specs=[VMEM] * 4,
        scratch_shapes=[pltpu.VMEM((F, MT, WIDE), f32), pltpu.SemaphoreType.DMA((2,))],
        name="pack0",
        compiler_params=params(),
    )(native)
    for q in range(2):
        if q:
            down, up, mine = pl.pallas_call(
                pack,
                out_shape=packed,
                in_specs=[VMEM],
                out_specs=[VMEM] * 3,
                name="pack1",
                compiler_params=params(),
                cost_estimate=pl.CostEstimate(flops=10**6, bytes_accessed=10**6, transcendentals=0),
            )(ham)
        plus.append(lax.ppermute(down, "gx", back))
        minus.append(lax.ppermute(up, "gx", ahead))
        own.append(mine)
    side = pl.pallas_call(
        side_kernel,
        out_shape=struct((ROWS, SIDE)),
        in_specs=[SMEM, VMEM, VMEM],
        out_specs=VMEM,
        name="side",
        compiler_params=params(),
    )(odd, *own)
    side = lax.ppermute(side, "gy", crossing)
    corners = []
    for q in range(2):
        x, i, near = pl.pallas_call(
            corner_kernel,
            out_shape=[struct((ROWS, CORNER)), struct((ROWS, CORNER)), struct((ROWS, NEAR))],
            in_specs=[SMEM, VMEM, VMEM, VMEM],
            out_specs=[VMEM] * 3,
            name=f"corner{q}",
            compiler_params=params(),
            cost_estimate=pl.CostEstimate(flops=(0, 40000000000)[q], bytes_accessed=(1, 10**8)[q], transcendentals=0),
        )(odd, own[q], plus[q], minus[q])
        corners.append(
            (lax.ppermute(x, "gy", crossing), lax.ppermute(i, "gy", inside), lax.ppermute(near, "gy", inside))
        )
    square = pltpu.VMEM((DIM, DIM), bf16)
    work = [
        pltpu.VMEM((LANES // 128, 10 * ROWS, 128), f32),
        pltpu.VMEM((DIM, DIM), f32),
        pltpu.VMEM((DIM // 128, LANES, 128), f32),
    ]
    margin, root_hi, root_lo = pl.pallas_call(
        root_kernel,
        out_shape=[struct((DIM, DIM)), struct((DIM, DIM), bf16), struct((DIM, DIM), bf16)],
        in_specs=[SMEM, SMEM] + [VMEM] * 7,
        out_specs=[VMEM] * 3,
        scratch_shapes=work + [square] * 4,
        name="inverse_root",
        compiler_params=params(),
        cost_estimate=pl.CostEstimate(flops=4 * 2 * DIM**3, bytes_accessed=2**23, transcendentals=0),
    )(odd, codes, own[0], plus[0], minus[0], side, *corners[0])
    folded = struct((ROWS + 8, 256))
    spread, up, mid, down = pl.pallas_call(
        density_kernel,
        out_shape=[struct((CODES * G, 128)), folded, struct((ROWS, 3 * TILE)), folded],
        in_specs=[SMEM, SMEM, SMEM] + [VMEM] * 10,
        out_specs=[VMEM] * 4,
        scratch_shapes=work
        + [square] * 6
        + [pltpu.VMEM((128, DIM), f32), pltpu.VMEM((DIM, 128), f32), pltpu.VMEM((3, ROWS, 128), f32)],
        name="density",
        compiler_params=params(),
        cost_estimate=pl.CostEstimate(flops=12 * 2 * DIM**3, bytes_accessed=2**23, transcendentals=0),
    )(odd, codes, chem_potential, own[1], plus[1], minus[1], side, *corners[1], margin, root_hi, root_lo)
    from_minus = lax.ppermute(up, "gx", ahead)
    from_plus = lax.ppermute(down, "gx", back)
    w = pl.pallas_call(
        own_kernel,
        out_shape=struct((LANES // 128, ROWS, 128)),
        in_specs=[VMEM],
        out_specs=VMEM,
        scratch_shapes=[pltpu.VMEM((LANES, 128), f32)],
        name="own",
        compiler_params=params(),
    )(spread)
    x, i = pl.pallas_call(
        turn_kernel,
        out_shape=[folded] * 2,
        in_specs=[VMEM] * 3,
        out_specs=[VMEM] * 2,
        name="turn",
        compiler_params=params(),
    )(mid, from_minus, from_plus)
    x = lax.ppermute(x, "gy", crossing)
    i = lax.ppermute(i, "gy", inside)
    out = pl.pallas_call(
        final_kernel,
        out_shape=struct((F, MT, WIDE)),
        in_specs=[SMEM] + [VMEM] * 6,
        out_specs=VMEM,
        name="symmetrize",
        compiler_params=params(),
    )(odd, w, mid, from_minus, from_plus, x, i)
    return jnp.transpose(out, (1, 0, 2))[None, None]


def solution(mesh):
    return jax.shard_map(
        shards,
        mesh=mesh,
        in_specs=(P("gx", "gy", None, None, None, None), P("gx", "gy", None), P()),
        out_specs=P("gx", "gy", None, None, None),
        check_vma=False,
    )
```
